256 devices in a mesh: ctx: 32 (over z, y_lo, core), head: 8 (over y_hi, x).
Axes of the slice: x: 4, y: 4 (y_hi: 2, y_lo: 2; y = y_hi * 2 + y_lo), z: 8, core: 2. Of those that a mesh axis runs over, the one named last changes fastest.
Arguments:
- queries: bfloat16 [4096, 5120], P('ctx', 'head'), may hold values from -80 to 80
- keys: bfloat16 [4096, 1024], P('ctx', 'head'), may hold values from -4 to 4
- values: bfloat16 [4096, 1024], P('ctx', 'head'), may hold values from -6 to 6
- out_grad: bfloat16 [4096, 5120], P('ctx', 'head'), may hold values from -6 to 6
- out_weight: bfloat16 [5120, 5120], P('head'), may hold values from -0.078125 to 0.078125
- seq_lengths: int32 [4], replicated, may hold values from 1 to 2048, as said below
- prompt_lengths: int32 [4], replicated, may hold values from 1 to 127
Outputs:
- query_grad: bfloat16 [4096, 5120], P('ctx', 'head')
- key_grad: bfloat16 [4096, 1024], P('ctx', 'head')
- value_grad: bfloat16 [4096, 1024], P('ctx', 'head')
The draws below stay inside these ranges and needn't reach their ends.
Inputs may be any that keep to these rules, and one draw needn't show every extreme that they name: `seq_lengths`: the lengths sum to 4096; the first is exactly 2048.
All inputs are finite; a program needn't handle non-finite values.
Results may differ from the reference program's by a relative error of at most 0.015.
Values may be sent and summed in bfloat16 or wider, within the bound.
No kernel may reach another device: no remote copies, remote signals or barrier semaphores. Data moves between devices by JAX's collectives and lax.ppermute only.
A program may use at most 64 MiB of HBM per device.

```python
import math
import jax
import jax.numpy as jnp
from jax import lax

D = 5120
HEADS_Q = 40
HEADS_KV = 8
HEAD_DIM = 128
TOK_DEV = 128
SEQS = 4
TOKENS = 4096


def shared_keys(key):
    drawn_keys = jax.random.truncated_normal(jax.random.fold_in(key, 11), -4.0, 4.0, (TOKENS, HEADS_KV * HEAD_DIM), jnp.float32)
    distance = 3 * TOKENS // 8
    places = jnp.arange(TOKENS, dtype=jnp.int32)
    copied = (places % 97 == 5) & (places >= distance) & (places < TOKENS // 2)
    blended = drawn_keys
    return jnp.where(copied[:, None], blended, drawn_keys)


def draw_keys(key, part):
    drawn_keys = shared_keys(key)
    return drawn_keys.astype(jnp.bfloat16)


def draw_queries(key, part):
    key = jax.random.fold_in(key, 5)
    fresh_rows = jax.random.truncated_normal(key, -4.0, 4.0, (TOKENS, HEADS_Q * HEAD_DIM), jnp.float32)
    return fresh_rows.astype(jnp.bfloat16)


def draw_seq_lengths(key, part):
    key = jax.random.fold_in(key, 7)
    half = TOKENS // 2
    inner = jnp.arange(1, half, dtype=jnp.int32)
    cuts = jnp.sort(jax.random.permutation(key, inner)[:SEQS - 2])
    edges = jnp.concatenate([jnp.zeros((1,), jnp.int32), cuts.astype(jnp.int32), jnp.full((1,), half, jnp.int32)])
    rest = (edges[1:] - edges[:-1]).astype(jnp.int32)
    return jnp.concatenate([jnp.full((1,), half, jnp.int32), rest])


def with_ends(result, stream_key, least, top_value):
    extent = result.shape
    place = [jax.random.randint(jax.random.fold_in(stream_key, axis), (), 0, extent[axis]) for axis in range(len(extent))]
    result = result.at[tuple(place)].set(least)
    longest = extent.index(max(extent))
    place[longest] = (place[longest] + 1) % extent[longest]
    return result.at[tuple(place)].set(top_value)


def shard_levels(own_key, extent, pieces, least, high):
    gain = 1.0
    for axis_at, blocks in pieces:
        heights = jax.random.uniform(jax.random.fold_in(jax.random.fold_in(own_key, 6), axis_at), (blocks,), jnp.float32, least / len(pieces), high / len(pieces))
        gain = gain * jnp.repeat(jnp.exp(heights), extent[axis_at] // blocks).reshape((-1,) + (1,) * (len(extent) - 1 - axis_at))
    return gain


def noise(stream_key, shape, deviation, most, pieces=(), kind=jnp.bfloat16):
    values = jax.random.normal(stream_key, shape, jnp.float32) * deviation
    if len(pieces) > 0:
        values = shard_levels(stream_key, shape, pieces, -0.22, 0.18) * values
    return jnp.clip(values, min=-most, max=most).astype(kind)


def setup_inputs(seed: int = 0) -> dict:
    key_of = jax.random.split(jax.random.key(seed), 8)
    queries = draw_queries(jax.random.fold_in(key_of[7], 71), 0)
    keys = draw_keys(jax.random.fold_in(key_of[7], 71), 0)
    values = noise(key_of[2], (TOKENS, HEADS_KV * HEAD_DIM), 1.0, 6.0, ((0, 32), (1, 8)))
    out_grad = noise(key_of[3], (TOKENS, D), 1.0, 6.0, ((0, 32), (1, 8)))
    out_weight = noise(key_of[4], (HEADS_Q * HEAD_DIM, D), D ** -0.5, 0.078125, ((0, 8),))
    seq_lengths = draw_seq_lengths(jax.random.fold_in(key_of[7], 71), 0)
    prompt_lengths = with_ends(jax.random.randint(key_of[6], (SEQS,), 1, TOK_DEV), jax.random.fold_in(key_of[6], 1), 1, TOK_DEV - 1).astype(jnp.int32)
    return dict(queries=queries, keys=keys, values=values, out_grad=out_grad, out_weight=out_weight, seq_lengths=seq_lengths, prompt_lengths=prompt_lengths)


NEG_LARGE = -1e+30

def segment_of(positions, bounds):
    return lax.optimization_barrier(jnp.sum((positions[:, None] >= bounds[None, :]).astype(jnp.int32), axis=1))

def layout(seq_lengths, prompt_lengths, positions):
    bounds = jnp.cumsum(seq_lengths).astype(jnp.int32)
    answer_start = bounds - seq_lengths + jnp.minimum(prompt_lengths, seq_lengths - 1)
    segment = segment_of(positions, bounds)
    labels = jnp.arange(bounds.shape[0], dtype=jnp.int32)
    picked = lax.optimization_barrier(jnp.sum(jnp.where(segment[:, None] == labels[None, :], answer_start[None, :], 0), axis=1))
    return (segment, positions >= picked)

def reference(queries, keys, values, out_grad, out_weight, seq_lengths, prompt_lengths):
    total = queries.shape[0]
    group = HEADS_Q // HEADS_KV
    scale = 1.0 / math.sqrt(HEAD_DIM)
    positions = jnp.arange(total, dtype=jnp.int32)
    segment, answer = layout(seq_lengths, prompt_lengths, positions)
    allowed = (positions[None, :] <= positions[:, None]) & (segment[None, :] == segment[:, None])
    summed = lax.dot_general(out_grad, out_weight, (((1,), (1,)), ((), ())), preferred_element_type=jnp.float32)
    grads = (summed * answer[:, None].astype(jnp.float32)).astype(jnp.bfloat16)
    query_heads = queries.reshape(total, HEADS_Q, HEAD_DIM).transpose(1, 0, 2)
    grad_heads = grads.reshape(total, HEADS_Q, HEAD_DIM).transpose(1, 0, 2)
    key_heads = jnp.repeat(keys.reshape(total, HEADS_KV, HEAD_DIM), group, axis=1).transpose(1, 0, 2)
    value_heads = jnp.repeat(values.reshape(total, HEADS_KV, HEAD_DIM), group, axis=1).transpose(1, 0, 2)

    def per_head(items):
        query, key_rows, value_rows, grad_rows = items
        scores = jnp.dot(query, key_rows.T, preferred_element_type=jnp.float32) * scale
        peak = lax.optimization_barrier(jnp.max(jnp.where(allowed, scores, NEG_LARGE), axis=1))
        mass = lax.optimization_barrier(jnp.sum(jnp.where(allowed, jnp.exp(scores - peak[:, None]), 0.0), axis=1))
        logsum = peak + jnp.log(mass)
        probs = jnp.where(allowed, jnp.exp(scores - logsum[:, None]), 0.0)
        dprobs = jnp.dot(grad_rows, value_rows.T, preferred_element_type=jnp.float32)
        delta = lax.optimization_barrier(jnp.sum(probs * dprobs, axis=1))
        dscores = (probs * (dprobs - delta[:, None])).astype(jnp.bfloat16)
        probs_half = probs.astype(jnp.bfloat16)
        dims = (((0,), (0,)), ((), ()))
        dvalue = lax.dot_general(probs_half, grad_rows, dims, preferred_element_type=jnp.float32)
        dkey = lax.dot_general(dscores, query, dims, preferred_element_type=jnp.float32) * scale
        dquery = jnp.dot(dscores, key_rows, preferred_element_type=jnp.float32) * scale
        return (dquery.astype(jnp.bfloat16), dkey, dvalue)
    dquery, dkey, dvalue = lax.map(per_head, (query_heads, key_heads, value_heads, grad_heads))
    query_grad = dquery.transpose(1, 0, 2).reshape(total, HEADS_Q * HEAD_DIM)
    key_grad = lax.optimization_barrier(jnp.sum(dkey.reshape(HEADS_KV, group, total, HEAD_DIM), axis=1))
    value_grad = lax.optimization_barrier(jnp.sum(dvalue.reshape(HEADS_KV, group, total, HEAD_DIM), axis=1))
    key_grad = key_grad.transpose(1, 0, 2).reshape(total, HEADS_KV * HEAD_DIM).astype(jnp.bfloat16)
    value_grad = value_grad.transpose(1, 0, 2).reshape(total, HEADS_KV * HEAD_DIM).astype(jnp.bfloat16)
    return (query_grad, key_grad, value_grad)
```

```python
import math

import jax
import jax.numpy as jnp
from jax import lax
from jax.experimental import pallas as pl
from jax.experimental.pallas import tpu as pltpu
from jax.sharding import PartitionSpec as P

HEADS_Q = 40
HEADS_KV = 8
HEAD_DIM = 128
GROUP = HEADS_Q // HEADS_KV
HALF = 16
TILES = 8
NEG = -1e30
SCALE = 1.0 / math.sqrt(HEAD_DIM)
LOG2_SCALE = SCALE * math.log2(math.e)
BF16 = jnp.bfloat16
F32 = jnp.float32
VMEM_LIMIT = 32 * 1024 * 1024
WIDE_LIMIT = 40 * 1024 * 1024


def ctx_swap(value, bits):
    count = lax.axis_size("ctx")
    return lax.ppermute(value, "ctx", [(i, i ^ bits) for i in range(count)])


def head_swap(value, bits):
    count = lax.axis_size("head")
    return lax.ppermute(value, "head", [(i, i ^ bits) for i in range(count)])


def dot_nn(a, b):
    return lax.dot_general(a, b, (((1,), (0,)), ((), ())), preferred_element_type=F32)


def dot_nt(a, b):
    return lax.dot_general(a, b, (((1,), (1,)), ((), ())), preferred_element_type=F32)


def heads(index):
    return slice(index * HEAD_DIM, (index + 1) * HEAD_DIM)


TILE_BLOCKS = (((0, 0), (1, 0)), ((0, 1), (1, 1)), ((0, 2), (0, 3)), ((1, 2), (1, 3)))


def tile_blocks(own, tile):
    return [own ^ (z * 4 + y * 2 + tile // 4) for y, z in TILE_BLOCKS[tile % 4]]


def own_geometry(geo_ref, count):
    place = lax.axis_index("ctx")
    own = place % HALF
    base = place - own
    low_block = jnp.maximum(jnp.min(geo_ref[0]) // count - base, 0)
    return place, own, base, low_block


def tile_active(own, low_block, tile):
    first, second = tile_blocks(own, tile)
    return ((first <= own) & (first >= low_block)) | ((second <= own) & (second >= low_block))


def fold_rows(values, reduce):
    rows, lanes = values.shape
    return reduce(values.reshape(rows // 8, 8, lanes), axis=0)


def prepare_kernel(lens_ref, prompts_ref, k_ref, v_ref, q_ref, kv_ref, qt_ref, qs_ref, geo_ref):
    kv_ref[:, :HEAD_DIM] = k_ref[...]
    kv_ref[:, HEAD_DIM:] = v_ref[...]
    for h in range(GROUP):
        qt_ref[:, heads(h)] = q_ref[:, heads(h)].T
        qs_ref[heads(h), :] = q_ref[:, heads(h)]
    rows, count = geo_ref.shape[1:]
    position = lax.axis_index("ctx") * count + lax.broadcasted_iota(jnp.int32, (rows, count), 1)
    start = jnp.int32(0)
    begin = jnp.zeros((rows, count), jnp.int32)
    answer_from = jnp.zeros((rows, count), jnp.int32)
    for s in range(lens_ref.shape[0]):
        answer = start + jnp.minimum(prompts_ref[s], lens_ref[s] - 1)
        begin = jnp.where(position >= start, start, begin)
        answer_from = jnp.where(position >= start, answer, answer_from)
        start = start + lens_ref[s]
    geo_ref[0] = begin
    geo_ref[1] = jnp.where(position >= answer_from, 1, 0)


def attend_kernel(geo_ref, w_ref, qt_ref, *refs):
    kv_refs = refs[:TILES]
    p_ref, o_ref, inv_ref, w_out, s_ref, m_ref, l_ref, sem = refs[TILES:]
    weights = pltpu.make_async_copy(w_ref, w_out, sem)
    weights.start()
    count = kv_refs[0].shape[0] // 2
    place, own, base, low_block = own_geometry(geo_ref, count)
    q_pos = place * count + lax.broadcasted_iota(jnp.int32, (count, count), 1)
    q_start = geo_ref[0, 0:1, :]
    m_ref[...] = jnp.full(m_ref.shape, NEG, F32)
    l_ref[...] = jnp.zeros(l_ref.shape, F32)
    o_ref[...] = jnp.zeros(o_ref.shape, F32)

    for tile in range(TILES):

        @pl.when(tile_active(own, low_block, tile))
        def _(tile=tile):
            biases = []
            for block in tile_blocks(own, tile):
                k_pos = (base + block) * count + lax.broadcasted_iota(jnp.int32, (count, count), 0)
                biases.append(jnp.where((k_pos <= q_pos) & (k_pos >= q_start), 0.0, NEG).astype(F32))
            bias = jnp.concatenate(biases, axis=0)
            keys = kv_refs[tile][:, :HEAD_DIM]
            for h in range(GROUP):
                scores = dot_nn(keys, qt_ref[:, heads(h)]) * LOG2_SCALE + bias
                s_ref[tile, :, heads(h)] = scores
                m_ref[:, heads(h)] = jnp.maximum(m_ref[:, heads(h)], fold_rows(scores, jnp.max))

    m_ref[...] = jnp.broadcast_to(jnp.max(m_ref[...], axis=0, keepdims=True), m_ref.shape)

    for tile in range(TILES):

        @pl.when(tile_active(own, low_block, tile))
        def _(tile=tile):
            values = kv_refs[tile][:, HEAD_DIM:].T
            for h in range(GROUP):
                probs = jnp.exp2(s_ref[tile, :, heads(h)] - m_ref[0:1, heads(h)])
                l_ref[:, heads(h)] = l_ref[:, heads(h)] + fold_rows(probs, jnp.sum)
                half = probs.astype(BF16)
                p_ref[tile, :, heads(h)] = half
                o_ref[:, heads(h)] += dot_nn(values, half)

    inverse = 1.0 / jnp.sum(l_ref[...], axis=0, keepdims=True)
    inv_ref[...] = jnp.broadcast_to(inverse, inv_ref.shape)
    weights.wait()


def tile_gradients(tile, p_ref, kv_ref, gt_ref, g_ref, qs_ref, delta_ref, ds_ref, dqt_ref, out):
    count = out.shape[2]
    keys, values = kv_ref[:, :HEAD_DIM], kv_ref[:, HEAD_DIM:]
    for h in range(GROUP):
        dprobs = dot_nn(values, gt_ref[:, heads(h)])
        probs = p_ref[tile, :, heads(h)].astype(F32)
        ds_ref[:, heads(h)] = (probs * (dprobs - delta_ref[0:1, heads(h)])).astype(BF16)
    dvalue = dot_nn(p_ref[tile], g_ref[...])
    dkey = dot_nn(ds_ref[...], qs_ref[...]) * SCALE
    dqt_ref[...] += dot_nn(keys.T, ds_ref[...])
    for n, (y, z) in enumerate(TILE_BLOCKS[tile % 4]):
        rows = slice(n * count, (n + 1) * count)
        out[y, z % 2, :, :HEAD_DIM] = dkey[rows].astype(out.dtype)
        out[y, z % 2, :, HEAD_DIM:] = dvalue[rows].astype(out.dtype)


def all_tiles(group, geo_ref, count, p_ref, kv_refs, gt_ref, g_ref, qs_ref, delta_ref, ds_ref, dqt_ref, keep_ref, send_ref):
    _, own, _, low_block = own_geometry(geo_ref, count)
    for core, out in ((1, send_ref), (0, keep_ref)):
        for n, member in enumerate(group):
            tile = core * 4 + member
            kv_ref = kv_refs[core * len(group) + n]
            active = tile_active(own, low_block, tile)

            @pl.when(active)
            def _(tile=tile, kv_ref=kv_ref, out=out):
                tile_gradients(tile, p_ref, kv_ref, gt_ref, g_ref, qs_ref, delta_ref, ds_ref, dqt_ref, out)

            @pl.when(jnp.logical_not(active))
            def _(tile=tile, out=out):
                for y, z in TILE_BLOCKS[tile % 4]:
                    out[y, z % 2] = jnp.zeros(out.shape[2:], out.dtype)


def far_kernel(group, geo_ref, w_ref, qs_ref, o_ref, inv_ref, p_ref, *refs):
    og_refs, kv_refs = refs[:4], refs[4 : 4 + 2 * len(group)]
    keep_ref, send_ref, gt_ref, g_ref, delta_ref, dqt_ref, ds_ref, acc_ref = refs[4 + 2 * len(group) :]
    _, count, width = og_refs[0].shape
    mine = lax.axis_index("head")
    parts = [(slot ^ (4 * n), slot, n) for slot in range(4) for n in range(2)]
    for n, (slot, array, half) in enumerate(parts):
        columns = pl.ds(pl.multiple_of((mine ^ slot) * width, HEAD_DIM), width)
        part = dot_nt(w_ref[:, columns], og_refs[array][half])
        if n == 0:
            acc_ref[...] = part
        else:
            acc_ref[...] += part
    answer = geo_ref[1, 0:1, :].astype(F32)
    for h in range(GROUP):
        inverse = inv_ref[0:1, heads(h)]
        grads = (acc_ref[heads(h), :] * answer).astype(BF16).astype(F32)
        scaled = (grads * inverse).astype(BF16)
        gt_ref[:, heads(h)] = scaled
        g_ref[heads(h), :] = scaled.T
        delta = jnp.sum(scaled.astype(F32) * (o_ref[:, heads(h)] * inverse), axis=0, keepdims=True)
        delta_ref[:, heads(h)] = jnp.broadcast_to(delta, (8, HEAD_DIM))
    dqt_ref[...] = jnp.zeros(dqt_ref.shape, F32)
    all_tiles(group, geo_ref, count, p_ref, kv_refs, gt_ref, g_ref, qs_ref, delta_ref, ds_ref, dqt_ref, keep_ref, send_ref)


def near_kernel(group, geo_ref, p_ref, gt_ref, g_ref, qs_ref, delta_ref, dqt_in, *refs):
    n_kv = 2 * len(group)
    kv_refs = refs[:n_kv]
    keep_ref, send_ref, dq_ref, ds_ref, dqt_ref = refs[n_kv:]
    count = dq_ref.shape[0]
    dqt_ref[...] = dqt_in[...]
    all_tiles(group, geo_ref, count, p_ref, kv_refs, gt_ref, g_ref, qs_ref, delta_ref, ds_ref, dqt_ref, keep_ref, send_ref)
    for h in range(GROUP):
        dq_ref[:, heads(h)] = (dqt_ref[:, heads(h)] * SCALE).T.astype(BF16)


VMEM_SPEC = pl.BlockSpec(memory_space=pltpu.VMEM)
SMEM_SPEC = pl.BlockSpec(memory_space=pltpu.SMEM)
ANY_SPEC = pl.BlockSpec(memory_space=pltpu.HBM)
PARAMS = pltpu.CompilerParams(vmem_limit_bytes=VMEM_LIMIT)


def prepare(seq_lengths, prompt_lengths, keys, values, queries):
    count, features = queries.shape
    return pl.pallas_call(
        prepare_kernel,
        out_shape=(
            jax.ShapeDtypeStruct((count, 2 * HEAD_DIM), BF16),
            jax.ShapeDtypeStruct((HEAD_DIM, features), BF16),
            jax.ShapeDtypeStruct((features, HEAD_DIM), BF16),
            jax.ShapeDtypeStruct((2, 8, count), jnp.int32),
        ),
        in_specs=[SMEM_SPEC] * 2 + [VMEM_SPEC] * 3,
        out_specs=(VMEM_SPEC,) * 4,
        name="prepare",
    )(seq_lengths, prompt_lengths, keys, values, queries)


def attend(geometry, weight, query_t, kv_tiles):
    _, features = query_t.shape
    keys = kv_tiles[0].shape[0]
    flops = 2 * TILES * keys * features * HEAD_DIM
    return pl.pallas_call(
        attend_kernel,
        out_shape=(
            jax.ShapeDtypeStruct((TILES, keys, features), BF16),
            jax.ShapeDtypeStruct((HEAD_DIM, features), F32),
            jax.ShapeDtypeStruct((8, features), F32),
            jax.ShapeDtypeStruct(weight.shape, BF16),
        ),
        in_specs=[VMEM_SPEC, ANY_SPEC] + [VMEM_SPEC] * (1 + TILES),
        out_specs=(VMEM_SPEC,) * 4,
        scratch_shapes=[
            pltpu.VMEM((TILES, keys, features), F32),
            pltpu.VMEM((8, features), F32),
            pltpu.VMEM((8, features), F32),
            pltpu.SemaphoreType.DMA,
        ],
        compiler_params=pltpu.CompilerParams(vmem_limit_bytes=WIDE_LIMIT),
        cost_estimate=pl.CostEstimate(
            flops=2 * flops, bytes_accessed=TILES * keys * features * 2, transcendentals=TILES * keys * features
        ),
        name="attend",
    )(geometry, weight, query_t, *kv_tiles)


def far_gradients(group, geometry, weight, query_s, attended, probs, blocks, kv_tiles):
    _, count, width = blocks[0].shape
    features = query_s.shape[0]
    keys = kv_tiles[0].shape[0]
    flops = 2 * len(kv_tiles) * keys * features * HEAD_DIM
    partial = (2, len(group), count, 2 * HEAD_DIM)

    def kernel(*refs):
        far_kernel(group, *refs)

    return pl.pallas_call(
        kernel,
        out_shape=(
            jax.ShapeDtypeStruct(partial, F32),
            jax.ShapeDtypeStruct(partial, BF16),
            jax.ShapeDtypeStruct((HEAD_DIM, features), BF16),
            jax.ShapeDtypeStruct((features, HEAD_DIM), BF16),
            jax.ShapeDtypeStruct((8, features), F32),
            jax.ShapeDtypeStruct((HEAD_DIM, features), F32),
        ),
        in_specs=[VMEM_SPEC] * (6 + len(blocks) + len(kv_tiles)),
        out_specs=(VMEM_SPEC,) * 6,
        scratch_shapes=[
            pltpu.VMEM((keys, features), BF16),
            pltpu.VMEM((features, count), F32),
        ],
        compiler_params=PARAMS,
        cost_estimate=pl.CostEstimate(
            flops=4 * flops + 2 * weight.size * count, bytes_accessed=2 * weight.size, transcendentals=0
        ),
        name="far_gradients",
    )(geometry, weight, query_s, *attended, probs, *blocks, *kv_tiles)


def near_gradients(group, geometry, probs, shared, kv_tiles):
    features, _ = shared[1].shape
    keys = kv_tiles[0].shape[0]
    count = keys // 2
    n_kv = len(kv_tiles)
    flops = 2 * n_kv * keys * features * HEAD_DIM
    partial = (2, len(group), count, 2 * HEAD_DIM)

    def kernel(*refs):
        near_kernel(group, *refs)

    return pl.pallas_call(
        kernel,
        out_shape=(
            jax.ShapeDtypeStruct(partial, F32),
            jax.ShapeDtypeStruct(partial, BF16),
            jax.ShapeDtypeStruct((count, features), BF16),
        ),
        in_specs=[VMEM_SPEC] * (7 + n_kv),
        out_specs=(VMEM_SPEC,) * 3,
        scratch_shapes=[pltpu.VMEM((keys, features), BF16), pltpu.VMEM((HEAD_DIM, features), F32)],
        compiler_params=PARAMS,
        cost_estimate=pl.CostEstimate(
            flops=4 * flops, bytes_accessed=2 * n_kv * keys * features, transcendentals=0
        ),
        name="near_gradients",
    )(geometry, probs, *shared, *kv_tiles)


def over_cores_and_y(keep, send):
    total = keep + ctx_swap(send, 1).astype(F32)
    return total[0] + ctx_swap(total[1].astype(BF16), 2).astype(F32)


def shards(queries, keys, values, out_grad, out_weight, seq_lengths, prompt_lengths):
    own, query_t, query_s, geometry = prepare(seq_lengths, prompt_lengths, keys, values, queries)
    og_pair = jnp.stack([out_grad, head_swap(out_grad, 4)])
    reach = jnp.concatenate([ctx_swap(own, 8), ctx_swap(own, 12)], axis=0)
    pair = jnp.concatenate([own, ctx_swap(own, 2)], axis=0)
    blocks = [og_pair] + [head_swap(og_pair, x) for x in (1, 2, 3)]
    tiles = [*lax.optimization_barrier((pair, ctx_swap(pair, 4))), *lax.optimization_barrier((reach, ctx_swap(reach, 2)))]
    tiles += [ctx_swap(tile, 1) for tile in tiles]
    far, near = (2, 3), (0, 1)
    probs, *attended, weight = attend(geometry, out_weight, query_t, tiles)
    far_keep, far_send, grads_t, grads, delta, dquery_t = far_gradients(
        far, geometry, weight, query_s, attended, probs, blocks, [tiles[4 * core + n] for core in (0, 1) for n in far]
    )
    shared = (grads_t, grads, query_s, delta, dquery_t)
    near_keep, near_send, query_grad = near_gradients(
        near, geometry, probs, shared, [tiles[4 * core + n] for core in (0, 1) for n in near]
    )
    far_total = over_cores_and_y(far_keep, far_send)
    near_total = over_cores_and_y(near_keep, near_send)
    kv_grad = near_total[0]
    kv_grad = kv_grad + ctx_swap(far_total[0].astype(BF16), 8).astype(F32)
    kv_grad = kv_grad + ctx_swap(far_total[1].astype(BF16), 12).astype(F32)
    kv_grad = kv_grad + ctx_swap(near_total[1].astype(BF16), 4).astype(F32)
    kv_grad = kv_grad.astype(BF16)
    return (query_grad, kv_grad[:, :HEAD_DIM], kv_grad[:, HEAD_DIM:])


def solution(mesh):
    return jax.shard_map(
        shards,
        mesh=mesh,
        in_specs=(
            P("ctx", "head"),
            P("ctx", "head"),
            P("ctx", "head"),
            P("ctx", "head"),
            P("head", None),
            P(),
            P(),
        ),
        out_specs=(P("ctx", "head"), P("ctx", "head"), P("ctx", "head")),
        check_vma=False,
    )
```

```python
import math

import jax
import jax.numpy as jnp
from jax import lax
from jax.experimental import pallas as pl
from jax.experimental.pallas import tpu as pltpu
from jax.sharding import PartitionSpec as P

HEADS_Q = 40
HEADS_KV = 8
HEAD_DIM = 128
GROUP = HEADS_Q // HEADS_KV
HALF = 16
TILES = 8
NEG = -1e30
SCALE = 1.0 / math.sqrt(HEAD_DIM)
LOG2_SCALE = SCALE * math.log2(math.e)
BF16 = jnp.bfloat16
F32 = jnp.float32
VMEM_LIMIT = 32 * 1024 * 1024
WIDE_LIMIT = 40 * 1024 * 1024


def ctx_swap(value, bits):
    count = lax.axis_size("ctx")
    return lax.ppermute(value, "ctx", [(i, i ^ bits) for i in range(count)])


def head_swap(value, bits):
    count = lax.axis_size("head")
    return lax.ppermute(value, "head", [(i, i ^ bits) for i in range(count)])


def dot_nn(a, b):
    return lax.dot_general(a, b, (((1,), (0,)), ((), ())), preferred_element_type=F32)


def dot_nt(a, b):
    return lax.dot_general(a, b, (((1,), (1,)), ((), ())), preferred_element_type=F32)


def heads(index):
    return slice(index * HEAD_DIM, (index + 1) * HEAD_DIM)


TILE_BLOCKS = (((0, 0), (1, 0)), ((0, 1), (1, 1)), ((0, 2), (0, 3)), ((1, 2), (1, 3)))


def tile_blocks(own, tile):
    return [own ^ (z * 4 + y * 2 + tile // 4) for y, z in TILE_BLOCKS[tile % 4]]


def own_geometry(qt_ref, count):
    geo = qt_ref[HEAD_DIM:, :count].astype(F32)
    place = lax.axis_index("ctx")
    own = place % HALF
    base = place - own
    low_block = jnp.maximum(jnp.min(geo[0:1]).astype(jnp.int32) - base, 0)
    return geo, place, own, base, low_block


def tile_active(own, low_block, tile):
    first, second = tile_blocks(own, tile)
    return ((first <= own) & (first >= low_block)) | ((second <= own) & (second >= low_block))


GEO_ROWS = 16
HEAD_RUNS = (slice(0, 256), slice(256, 512), slice(512, 640))


def fold_rows(values, reduce):
    rows, lanes = values.shape
    return reduce(values.reshape(rows // 8, 8, lanes), axis=0)


def prepare_kernel(lens_ref, prompts_ref, k_ref, v_ref, q_ref, kv_ref, qt_ref, qs_ref):
    kv_ref[:, :HEAD_DIM] = k_ref[...]
    kv_ref[:, HEAD_DIM:] = v_ref[...]
    for h in range(GROUP):
        qt_ref[:HEAD_DIM, heads(h)] = q_ref[:, heads(h)].T
        qs_ref[heads(h), :] = q_ref[:, heads(h)]
    rows, count = GEO_ROWS, q_ref.shape[0]
    position = lax.axis_index("ctx") * count + lax.broadcasted_iota(jnp.int32, (rows, count), 1)
    start = jnp.int32(0)
    begin = jnp.zeros((rows, count), jnp.int32)
    answer_from = jnp.zeros((rows, count), jnp.int32)
    for s in range(lens_ref.shape[0]):
        answer = start + jnp.minimum(prompts_ref[s], lens_ref[s] - 1)
        begin = jnp.where(position >= start, start, begin)
        answer_from = jnp.where(position >= start, answer, answer_from)
        start = start + lens_ref[s]
    kind = lax.broadcasted_iota(jnp.int32, (rows, count), 0)
    answer = jnp.where(position >= answer_from, 1, 0)
    small = jnp.where(kind == 0, begin // count, jnp.where(kind == 1, begin % count, answer))
    qt_ref[HEAD_DIM:, :count] = small.astype(F32).astype(BF16)
    qt_ref[HEAD_DIM:, count:] = jnp.zeros((rows, qt_ref.shape[1] - count), BF16)


def attend_kernel(w_ref, qt_ref, *refs):
    kv_refs = refs[:TILES]
    p_ref, o_ref, inv_ref, w_out, s_ref, m_ref, l_ref, sem = refs[TILES:]
    weights = pltpu.make_async_copy(w_ref, w_out, sem)
    weights.start()
    count = kv_refs[0].shape[0] // 2
    geo, place, own, base, low_block = own_geometry(qt_ref, count)
    q_pos = place * count + lax.broadcasted_iota(jnp.int32, (count, count), 1)
    q_start = (geo[0:1] * count + geo[1:2]).astype(jnp.int32)
    m_ref[...] = jnp.full(m_ref.shape, NEG, F32)
    l_ref[...] = jnp.zeros(l_ref.shape, F32)
    o_ref[...] = jnp.zeros(o_ref.shape, F32)

    for tile in range(TILES):

        @pl.when(tile_active(own, low_block, tile))
        def _(tile=tile):
            for n, block in enumerate(tile_blocks(own, tile)):
                rows = slice(n * count, (n + 1) * count)
                k_pos = (base + block) * count + lax.broadcasted_iota(jnp.int32, (count, count), 0)
                bias = jnp.where((k_pos <= q_pos) & (k_pos >= q_start), 0.0, NEG).astype(F32)
                keys = kv_refs[tile][rows, :HEAD_DIM]
                for run in HEAD_RUNS:
                    wide = (run.stop - run.start) // HEAD_DIM
                    scores = dot_nn(keys, qt_ref[:HEAD_DIM, run]) * LOG2_SCALE + jnp.concatenate([bias] * wide, axis=1)
                    s_ref[tile, rows, run] = scores
                    m_ref[:, run] = jnp.maximum(m_ref[:, run], fold_rows(scores, jnp.max))

    m_ref[...] = jnp.broadcast_to(jnp.max(m_ref[...], axis=0, keepdims=True), m_ref.shape)

    for tile in range(TILES):

        @pl.when(tile_active(own, low_block, tile))
        def _(tile=tile):
            values = kv_refs[tile][:, HEAD_DIM:].T
            for run in HEAD_RUNS:
                for n in range(2):
                    rows = slice(n * count, (n + 1) * count)
                    probs = jnp.exp2(s_ref[tile, rows, run] - m_ref[0:1, run])
                    l_ref[:, run] = l_ref[:, run] + fold_rows(probs, jnp.sum)
                    p_ref[tile, rows, run] = probs.astype(BF16)
                o_ref[:, run] += dot_nn(values, p_ref[tile, :, run])

    inverse = 1.0 / jnp.sum(l_ref[...], axis=0, keepdims=True)
    inv_ref[...] = jnp.broadcast_to(inverse, inv_ref.shape)
    weights.wait()


def tile_gradients(tile, p_ref, kv_ref, gt_ref, g_ref, qs_ref, delta_ref, ds_ref, dqt_ref, out):
    count = out.shape[2]
    keys, values = kv_ref[:, :HEAD_DIM], kv_ref[:, HEAD_DIM:]
    for run in HEAD_RUNS:
        for n in range(2):
            rows = slice(n * count, (n + 1) * count)
            dprobs = dot_nn(values[rows], gt_ref[:, run])
            probs = p_ref[tile, rows, run].astype(F32)
            ds_ref[rows, run] = (probs * (dprobs - delta_ref[0:1, run])).astype(BF16)
    dvalue = dot_nn(p_ref[tile], g_ref[...])
    dkey = dot_nn(ds_ref[...], qs_ref[...]) * SCALE
    dqt_ref[...] += dot_nn(keys.T, ds_ref[...])
    for n, (y, z) in enumerate(TILE_BLOCKS[tile % 4]):
        rows = slice(n * count, (n + 1) * count)
        out[y, z % 2, :, :HEAD_DIM] = dkey[rows].astype(out.dtype)
        out[y, z % 2, :, HEAD_DIM:] = dvalue[rows].astype(out.dtype)


def all_tiles(group, qt_ref, count, p_ref, kv_refs, gt_ref, g_ref, qs_ref, delta_ref, ds_ref, dqt_ref, keep_ref, send_ref):
    _, _, own, _, low_block = own_geometry(qt_ref, count)
    for core, out in ((1, send_ref), (0, keep_ref)):
        for n, member in enumerate(group):
            tile = core * 4 + member
            kv_ref = kv_refs[core * len(group) + n]
            active = tile_active(own, low_block, tile)

            @pl.when(active)
            def _(tile=tile, kv_ref=kv_ref, out=out):
                tile_gradients(tile, p_ref, kv_ref, gt_ref, g_ref, qs_ref, delta_ref, ds_ref, dqt_ref, out)

            @pl.when(jnp.logical_not(active))
            def _(tile=tile, out=out):
                for y, z in TILE_BLOCKS[tile % 4]:
                    out[y, z % 2] = jnp.zeros(out.shape[2:], out.dtype)


def far_kernel(group, qt_ref, w_ref, qs_ref, o_ref, inv_ref, p_ref, *refs):
    og_refs, kv_refs = refs[:5], refs[5 : 5 + 2 * len(group)]
    keep_ref, send_ref, gt_ref, g_ref, delta_ref, dqt_ref, ds_ref, acc_ref = refs[5 + 2 * len(group) :]
    _, count, width = og_refs[0].shape
    mine = lax.axis_index("head")
    parts = [(0, og_refs[0][0]), (4, og_refs[0][1]), (2, og_refs[3][...]), (6, og_refs[4][...])]
    parts += [(1, og_refs[1][0]), (5, og_refs[1][1]), (3, og_refs[2][0]), (7, og_refs[2][1])]
    for n, (slot, block) in enumerate(parts):
        columns = pl.ds(pl.multiple_of((mine ^ slot) * width, HEAD_DIM), width)
        part = dot_nt(w_ref[:, columns], block)
        if n == 0:
            acc_ref[...] = part
        else:
            acc_ref[...] += part
    answer = qt_ref[HEAD_DIM:, :count].astype(F32)[2:3]
    for h in range(GROUP):
        inverse = inv_ref[0:1, heads(h)]
        grads = (acc_ref[heads(h), :] * answer).astype(BF16).astype(F32)
        scaled = (grads * inverse).astype(BF16)
        gt_ref[:, heads(h)] = scaled
        g_ref[heads(h), :] = scaled.T
        delta = jnp.sum(scaled.astype(F32) * (o_ref[:, heads(h)] * inverse), axis=0, keepdims=True)
        delta_ref[:, heads(h)] = jnp.broadcast_to(delta, (8, HEAD_DIM))
    dqt_ref[...] = jnp.zeros(dqt_ref.shape, F32)
    all_tiles(group, qt_ref, count, p_ref, kv_refs, gt_ref, g_ref, qs_ref, delta_ref, ds_ref, dqt_ref, keep_ref, send_ref)


def near_kernel(group, qt_ref, p_ref, gt_ref, g_ref, qs_ref, delta_ref, dqt_in, *refs):
    n_kv = 2 * len(group)
    kv_refs = refs[:n_kv]
    keep_ref, send_ref, dq_ref, ds_ref, dqt_ref = refs[n_kv:]
    count = dq_ref.shape[0]
    dqt_ref[...] = dqt_in[...]
    all_tiles(group, qt_ref, count, p_ref, kv_refs, gt_ref, g_ref, qs_ref, delta_ref, ds_ref, dqt_ref, keep_ref, send_ref)
    for h in range(GROUP):
        dq_ref[:, heads(h)] = (dqt_ref[:, heads(h)] * SCALE).T.astype(BF16)


VMEM_SPEC = pl.BlockSpec(memory_space=pltpu.VMEM)
SMEM_SPEC = pl.BlockSpec(memory_space=pltpu.SMEM)
ANY_SPEC = pl.BlockSpec(memory_space=pltpu.HBM)
PARAMS = pltpu.CompilerParams(vmem_limit_bytes=VMEM_LIMIT)


def prepare(seq_lengths, prompt_lengths, keys, values, queries):
    count, features = queries.shape
    return pl.pallas_call(
        prepare_kernel,
        out_shape=(
            jax.ShapeDtypeStruct((count, 2 * HEAD_DIM), BF16),
            jax.ShapeDtypeStruct((HEAD_DIM + GEO_ROWS, features), BF16),
            jax.ShapeDtypeStruct((features, HEAD_DIM), BF16),
        ),
        in_specs=[SMEM_SPEC] * 2 + [VMEM_SPEC] * 3,
        out_specs=(VMEM_SPEC,) * 3,
        name="prepare",
    )(seq_lengths, prompt_lengths, keys, values, queries)


def attend(weight, query_t, kv_tiles):
    _, features = query_t.shape
    keys = kv_tiles[0].shape[0]
    flops = 2 * TILES * keys * features * HEAD_DIM
    return pl.pallas_call(
        attend_kernel,
        out_shape=(
            jax.ShapeDtypeStruct((TILES, keys, features), BF16),
            jax.ShapeDtypeStruct((HEAD_DIM, features), F32),
            jax.ShapeDtypeStruct((8, features), F32),
            jax.ShapeDtypeStruct(weight.shape, BF16),
        ),
        in_specs=[ANY_SPEC] + [VMEM_SPEC] * (1 + TILES),
        out_specs=(VMEM_SPEC,) * 4,
        scratch_shapes=[
            pltpu.VMEM((TILES, keys, features), F32),
            pltpu.VMEM((8, features), F32),
            pltpu.VMEM((8, features), F32),
            pltpu.SemaphoreType.DMA,
        ],
        compiler_params=pltpu.CompilerParams(vmem_limit_bytes=WIDE_LIMIT),
        cost_estimate=pl.CostEstimate(
            flops=2 * flops, bytes_accessed=TILES * keys * features * 2, transcendentals=TILES * keys * features
        ),
        name="attend",
    )(weight, query_t, *kv_tiles)


def far_gradients(group, query_t, weight, query_s, attended, probs, blocks, kv_tiles):
    _, count, width = blocks[0].shape
    features = query_s.shape[0]
    keys = kv_tiles[0].shape[0]
    flops = 2 * len(kv_tiles) * keys * features * HEAD_DIM
    partial = (2, len(group), count, 2 * HEAD_DIM)

    def kernel(*refs):
        far_kernel(group, *refs)

    return pl.pallas_call(
        kernel,
        out_shape=(
            jax.ShapeDtypeStruct(partial, F32),
            jax.ShapeDtypeStruct(partial, BF16),
            jax.ShapeDtypeStruct((HEAD_DIM, features), BF16),
            jax.ShapeDtypeStruct((features, HEAD_DIM), BF16),
            jax.ShapeDtypeStruct((8, features), F32),
            jax.ShapeDtypeStruct((HEAD_DIM, features), F32),
        ),
        in_specs=[VMEM_SPEC] * (6 + len(blocks) + len(kv_tiles)),
        out_specs=(VMEM_SPEC,) * 6,
        scratch_shapes=[
            pltpu.VMEM((keys, features), BF16),
            pltpu.VMEM((features, count), F32),
        ],
        compiler_params=PARAMS,
        cost_estimate=pl.CostEstimate(
            flops=4 * flops + 2 * weight.size * count, bytes_accessed=2 * weight.size, transcendentals=0
        ),
        name="far_gradients",
    )(query_t, weight, query_s, *attended, probs, *blocks, *kv_tiles)


def near_gradients(group, query_t, probs, shared, kv_tiles):
    features, _ = shared[1].shape
    keys = kv_tiles[0].shape[0]
    count = keys // 2
    n_kv = len(kv_tiles)
    flops = 2 * n_kv * keys * features * HEAD_DIM
    partial = (2, len(group), count, 2 * HEAD_DIM)

    def kernel(*refs):
        near_kernel(group, *refs)

    return pl.pallas_call(
        kernel,
        out_shape=(
            jax.ShapeDtypeStruct(partial, F32),
            jax.ShapeDtypeStruct(partial, BF16),
            jax.ShapeDtypeStruct((count, features), BF16),
        ),
        in_specs=[VMEM_SPEC] * (7 + n_kv),
        out_specs=(VMEM_SPEC,) * 3,
        scratch_shapes=[pltpu.VMEM((keys, features), BF16), pltpu.VMEM((HEAD_DIM, features), F32)],
        compiler_params=PARAMS,
        cost_estimate=pl.CostEstimate(
            flops=4 * flops, bytes_accessed=2 * n_kv * keys * features, transcendentals=0
        ),
        name="near_gradients",
    )(query_t, probs, *shared, *kv_tiles)


def over_cores_and_y(keep, send):
    total = keep + ctx_swap(send, 1).astype(F32)
    return total[0] + ctx_swap(total[1].astype(BF16), 2).astype(F32)


def shards(queries, keys, values, out_grad, out_weight, seq_lengths, prompt_lengths):
    own, query_t, query_s = prepare(seq_lengths, prompt_lengths, keys, values, queries)
    own, out_grad = lax.optimization_barrier((own, out_grad))
    og_pair = jnp.stack([out_grad, head_swap(out_grad, 4)])
    reach = jnp.concatenate([ctx_swap(own, 8), ctx_swap(own, 12)], axis=0)
    pair = jnp.concatenate([own, ctx_swap(own, 2)], axis=0)
    across = head_swap(out_grad, 2)
    both = head_swap(across, 4)
    blocks = [og_pair, head_swap(og_pair, 1), head_swap(og_pair, 3), across, both]
    tiles = [*lax.optimization_barrier((pair, ctx_swap(pair, 4))), *lax.optimization_barrier((reach, ctx_swap(reach, 2)))]
    tiles += [ctx_swap(tile, 1) for tile in tiles]
    far, near = (2, 3), (0, 1)
    probs, *attended, weight = attend(out_weight, query_t, tiles)
    far_keep, far_send, grads_t, grads, delta, dquery_t = far_gradients(
        far, query_t, weight, query_s, attended, probs, blocks, [tiles[4 * core + n] for core in (0, 1) for n in far]
    )
    shared = (grads_t, grads, query_s, delta, dquery_t)
    near_keep, near_send, query_grad = near_gradients(
        near, query_t, probs, shared, [tiles[4 * core + n] for core in (0, 1) for n in near]
    )
    far_received, near_send = lax.optimization_barrier((ctx_swap(far_send, 1), near_send))
    far_sum = far_keep + far_received.astype(F32)
    near_sum = near_keep + ctx_swap(near_send, 1).astype(F32)
    far_across = ctx_swap(far_sum[1].astype(BF16), 2)
    near_payload = near_sum[1].astype(BF16)
    far_across, _ = lax.optimization_barrier((far_across, near_payload))
    far_total = far_sum[0] + far_across.astype(F32)
    near_total = near_sum[0] + ctx_swap(near_payload, 2).astype(F32)
    beyond = lax.optimization_barrier((far_total[0].astype(BF16), far_total[1].astype(BF16)))
    near_total_own, beside = lax.optimization_barrier((near_total[0], near_total[1].astype(BF16)))
    received = [near_total_own, ctx_swap(beyond[0], 8), ctx_swap(beyond[1], 12), ctx_swap(beside, 4)]
    parts = [slice(0, HEAD_DIM), slice(HEAD_DIM, 2 * HEAD_DIM)]
    key_grad, value_grad = [sum(array[:, p].astype(F32) for array in received).astype(BF16) for p in parts]
    return (query_grad, key_grad, value_grad)


def solution(mesh):
    return jax.shard_map(
        shards,
        mesh=mesh,
        in_specs=(
            P("ctx", "head"),
            P("ctx", "head"),
            P("ctx", "head"),
            P("ctx", "head"),
            P("head", None),
            P(),
            P(),
        ),
        out_specs=(P("ctx", "head"), P("ctx", "head"), P("ctx", "head")),
        check_vma=False,
    )
```

```python
import math

import jax
import jax.numpy as jnp
from jax import lax
from jax.experimental import pallas as pl
from jax.experimental.pallas import tpu as pltpu
from jax.sharding import PartitionSpec as P

HEADS_Q = 40
HEADS_KV = 8
HEAD_DIM = 128
GROUP = HEADS_Q // HEADS_KV
HALF = 16
TILES = 8
NEG = -1e30
SCALE = 1.0 / math.sqrt(HEAD_DIM)
LOG2_SCALE = SCALE * math.log2(math.e)
BF16 = jnp.bfloat16
F32 = jnp.float32
VMEM_LIMIT = 32 * 1024 * 1024
WIDE_LIMIT = 40 * 1024 * 1024


def ctx_swap(value, bits):
    count = lax.axis_size("ctx")
    return lax.ppermute(value, "ctx", [(i, i ^ bits) for i in range(count)])


def send_back(value, bits):
    count = lax.axis_size("ctx")
    return lax.ppermute(value, "ctx", [(i, i ^ bits) for i in range(count) if i ^ bits < i])


def head_swap(value, bits):
    count = lax.axis_size("head")
    return lax.ppermute(value, "head", [(i, i ^ bits) for i in range(count)])


def dot_nn(a, b):
    return lax.dot_general(a, b, (((1,), (0,)), ((), ())), preferred_element_type=F32)


def dot_nt(a, b):
    return lax.dot_general(a, b, (((1,), (1,)), ((), ())), preferred_element_type=F32)


def heads(index):
    return slice(index * HEAD_DIM, (index + 1) * HEAD_DIM)


TILE_BLOCKS = (((0, 0), (1, 0)), ((0, 1), (1, 1)), ((0, 2), (0, 3)), ((1, 2), (1, 3)))


def tile_blocks(own, tile):
    return [own ^ (z * 4 + y * 2 + tile // 4) for y, z in TILE_BLOCKS[tile % 4]]


def own_geometry(qt_ref, count):
    geo = qt_ref[HEAD_DIM:, :count].astype(F32)
    place = lax.axis_index("ctx")
    own = place % HALF
    base = place - own
    low_block = jnp.maximum(jnp.min(geo[0:1]).astype(jnp.int32) - base, 0)
    return geo, place, own, base, low_block


def tile_active(own, low_block, tile):
    first, second = tile_blocks(own, tile)
    return ((first <= own) & (first >= low_block)) | ((second <= own) & (second >= low_block))


GEO_ROWS = 16
HEAD_RUNS = (slice(0, 256), slice(256, 512), slice(512, 640))


def fold_rows(values, reduce):
    rows, lanes = values.shape
    return reduce(values.reshape(rows // 8, 8, lanes), axis=0)


def prepare_kernel(lens_ref, prompts_ref, k_ref, v_ref, q_ref, kv_ref, qt_ref, qs_ref):
    kv_ref[:, :HEAD_DIM] = k_ref[...]
    kv_ref[:, HEAD_DIM:] = v_ref[...]
    for h in range(GROUP):
        qt_ref[:HEAD_DIM, heads(h)] = q_ref[:, heads(h)].T
        qs_ref[heads(h), :] = q_ref[:, heads(h)]
    rows, count = GEO_ROWS, q_ref.shape[0]
    position = lax.axis_index("ctx") * count + lax.broadcasted_iota(jnp.int32, (rows, count), 1)
    start = jnp.int32(0)
    begin = jnp.zeros((rows, count), jnp.int32)
    answer_from = jnp.zeros((rows, count), jnp.int32)
    for s in range(lens_ref.shape[0]):
        answer = start + jnp.minimum(prompts_ref[s], lens_ref[s] - 1)
        begin = jnp.where(position >= start, start, begin)
        answer_from = jnp.where(position >= start, answer, answer_from)
        start = start + lens_ref[s]
    kind = lax.broadcasted_iota(jnp.int32, (rows, count), 0)
    answer = jnp.where(position >= answer_from, 1, 0)
    small = jnp.where(kind == 0, begin // count, jnp.where(kind == 1, begin % count, answer))
    qt_ref[HEAD_DIM:, :count] = small.astype(F32).astype(BF16)
    qt_ref[HEAD_DIM:, count:] = jnp.zeros((rows, qt_ref.shape[1] - count), BF16)


def attend_kernel(w_ref, qt_ref, *refs):
    kv_refs = refs[:TILES]
    p_ref, o_ref, inv_ref, w_out, s_ref, m_ref, l_ref, sem = refs[TILES:]
    weights = pltpu.make_async_copy(w_ref, w_out, sem)
    weights.start()
    count = kv_refs[0].shape[0] // 2
    geo, place, own, base, low_block = own_geometry(qt_ref, count)
    q_pos = place * count + lax.broadcasted_iota(jnp.int32, (count, count), 1)
    q_start = (geo[0:1] * count + geo[1:2]).astype(jnp.int32)
    m_ref[...] = jnp.full(m_ref.shape, NEG, F32)
    l_ref[...] = jnp.zeros(l_ref.shape, F32)
    o_ref[...] = jnp.zeros(o_ref.shape, F32)

    for tile in range(TILES):

        @pl.when(tile_active(own, low_block, tile))
        def _(tile=tile):
            for n, block in enumerate(tile_blocks(own, tile)):
                rows = slice(n * count, (n + 1) * count)
                k_pos = (base + block) * count + lax.broadcasted_iota(jnp.int32, (count, count), 0)
                bias = jnp.where((k_pos <= q_pos) & (k_pos >= q_start), 0.0, NEG).astype(F32)
                keys = kv_refs[tile][rows, :HEAD_DIM]
                for run in HEAD_RUNS:
                    wide = (run.stop - run.start) // HEAD_DIM
                    scores = dot_nn(keys, qt_ref[:HEAD_DIM, run]) * LOG2_SCALE + jnp.concatenate([bias] * wide, axis=1)
                    s_ref[tile, rows, run] = scores
                    m_ref[:, run] = jnp.maximum(m_ref[:, run], fold_rows(scores, jnp.max))

    m_ref[...] = jnp.broadcast_to(jnp.max(m_ref[...], axis=0, keepdims=True), m_ref.shape)

    for tile in range(TILES):

        @pl.when(tile_active(own, low_block, tile))
        def _(tile=tile):
            values = kv_refs[tile][:, HEAD_DIM:].T
            for run in HEAD_RUNS:
                for n in range(2):
                    rows = slice(n * count, (n + 1) * count)
                    probs = jnp.exp2(s_ref[tile, rows, run] - m_ref[0:1, run])
                    l_ref[:, run] = l_ref[:, run] + fold_rows(probs, jnp.sum)
                    p_ref[tile, rows, run] = probs.astype(BF16)
                o_ref[:, run] += dot_nn(values, p_ref[tile, :, run])

    inverse = 1.0 / jnp.sum(l_ref[...], axis=0, keepdims=True)
    inv_ref[...] = jnp.broadcast_to(inverse, inv_ref.shape)
    weights.wait()


def tile_gradients(tile, p_ref, kv_ref, gt_ref, g_ref, qs_ref, delta_ref, ds_ref, dqt_ref, out):
    count = out.shape[2]
    keys, values = kv_ref[:, :HEAD_DIM], kv_ref[:, HEAD_DIM:]
    for run in HEAD_RUNS:
        for n in range(2):
            rows = slice(n * count, (n + 1) * count)
            dprobs = dot_nn(values[rows], gt_ref[:, run])
            probs = p_ref[tile, rows, run].astype(F32)
            ds_ref[rows, run] = (probs * (dprobs - delta_ref[0:1, run])).astype(BF16)
    dvalue = dot_nn(p_ref[tile], g_ref[...])
    dkey = dot_nn(ds_ref[...], qs_ref[...]) * SCALE
    dqt_ref[...] += dot_nn(keys.T, ds_ref[...])
    for n, (y, z) in enumerate(TILE_BLOCKS[tile % 4]):
        rows = slice(n * count, (n + 1) * count)
        out[y, z % 2, :, :HEAD_DIM] = dkey[rows].astype(out.dtype)
        out[y, z % 2, :, HEAD_DIM:] = dvalue[rows].astype(out.dtype)


def all_tiles(outs, group, qt_ref, count, p_ref, kv_refs, gt_ref, g_ref, qs_ref, delta_ref, ds_ref, dqt_ref):
    _, _, own, _, low_block = own_geometry(qt_ref, count)
    for n_core, (core, out) in enumerate(outs):
        for n, member in enumerate(group):
            tile = core * 4 + member
            kv_ref = kv_refs[n_core * len(group) + n]
            active = tile_active(own, low_block, tile)

            @pl.when(active)
            def _(tile=tile, kv_ref=kv_ref, out=out):
                tile_gradients(tile, p_ref, kv_ref, gt_ref, g_ref, qs_ref, delta_ref, ds_ref, dqt_ref, out)

            @pl.when(jnp.logical_not(active))
            def _(tile=tile, out=out):
                for y, z in TILE_BLOCKS[tile % 4]:
                    out[y, z % 2] = jnp.zeros(out.shape[2:], out.dtype)


def far_kernel(group, qt_ref, w_ref, qs_ref, o_ref, inv_ref, p_ref, *refs):
    og_refs, kv_refs = refs[:5], refs[5 : 5 + 2 * len(group)]
    keep_ref, send_ref, gt_ref, g_ref, delta_ref, dqt_ref, ds_ref, acc_ref = refs[5 + 2 * len(group) :]
    _, count, width = og_refs[0].shape
    mine = lax.axis_index("head")
    parts = [(0, og_refs[0][0]), (4, og_refs[0][1]), (2, og_refs[3][...]), (6, og_refs[4][...])]
    parts += [(1, og_refs[1][0]), (5, og_refs[1][1]), (3, og_refs[2][0]), (7, og_refs[2][1])]
    for n, (slot, block) in enumerate(parts):
        columns = pl.ds(pl.multiple_of((mine ^ slot) * width, HEAD_DIM), width)
        part = dot_nt(w_ref[:, columns], block)
        if n == 0:
            acc_ref[...] = part
        else:
            acc_ref[...] += part
    answer = qt_ref[HEAD_DIM:, :count].astype(F32)[2:3]
    for h in range(GROUP):
        inverse = inv_ref[0:1, heads(h)]
        grads = (acc_ref[heads(h), :] * answer).astype(BF16).astype(F32)
        scaled = (grads * inverse).astype(BF16)
        gt_ref[:, heads(h)] = scaled
        g_ref[heads(h), :] = scaled.T
        delta = jnp.sum(scaled.astype(F32) * (o_ref[:, heads(h)] * inverse), axis=0, keepdims=True)
        delta_ref[:, heads(h)] = jnp.broadcast_to(delta, (8, HEAD_DIM))
    dqt_ref[...] = jnp.zeros(dqt_ref.shape, F32)
    outs = ((1, send_ref), (0, keep_ref))
    all_tiles(outs, group, qt_ref, count, p_ref, kv_refs, gt_ref, g_ref, qs_ref, delta_ref, ds_ref, dqt_ref)


def near_kernel(core, group, qt_ref, p_ref, gt_ref, g_ref, qs_ref, delta_ref, dqt_in, *refs):
    kv_refs = refs[: len(group)]
    out_ref, result_ref, ds_ref, dqt_ref = refs[len(group) :]
    count = out_ref.shape[2]
    dqt_ref[...] = dqt_in[...]
    all_tiles(((core, out_ref),), group, qt_ref, count, p_ref, kv_refs, gt_ref, g_ref, qs_ref, delta_ref, ds_ref, dqt_ref)
    if core == 1:
        result_ref[...] = dqt_ref[...]
    else:
        for h in range(GROUP):
            result_ref[:, heads(h)] = (dqt_ref[:, heads(h)] * SCALE).T.astype(BF16)


VMEM_SPEC = pl.BlockSpec(memory_space=pltpu.VMEM)
SMEM_SPEC = pl.BlockSpec(memory_space=pltpu.SMEM)
ANY_SPEC = pl.BlockSpec(memory_space=pltpu.HBM)
PARAMS = pltpu.CompilerParams(vmem_limit_bytes=VMEM_LIMIT)


def prepare(seq_lengths, prompt_lengths, keys, values, queries):
    count, features = queries.shape
    return pl.pallas_call(
        prepare_kernel,
        out_shape=(
            jax.ShapeDtypeStruct((count, 2 * HEAD_DIM), BF16),
            jax.ShapeDtypeStruct((HEAD_DIM + GEO_ROWS, features), BF16),
            jax.ShapeDtypeStruct((features, HEAD_DIM), BF16),
        ),
        in_specs=[SMEM_SPEC] * 2 + [VMEM_SPEC] * 3,
        out_specs=(VMEM_SPEC,) * 3,
        name="prepare",
    )(seq_lengths, prompt_lengths, keys, values, queries)


def attend(weight, query_t, kv_tiles):
    _, features = query_t.shape
    keys = kv_tiles[0].shape[0]
    flops = 2 * TILES * keys * features * HEAD_DIM
    return pl.pallas_call(
        attend_kernel,
        out_shape=(
            jax.ShapeDtypeStruct((TILES, keys, features), BF16),
            jax.ShapeDtypeStruct((HEAD_DIM, features), F32),
            jax.ShapeDtypeStruct((8, features), F32),
            jax.ShapeDtypeStruct(weight.shape, BF16),
        ),
        in_specs=[ANY_SPEC] + [VMEM_SPEC] * (1 + TILES),
        out_specs=(VMEM_SPEC,) * 4,
        scratch_shapes=[
            pltpu.VMEM((TILES, keys, features), F32),
            pltpu.VMEM((8, features), F32),
            pltpu.VMEM((8, features), F32),
            pltpu.SemaphoreType.DMA,
        ],
        compiler_params=pltpu.CompilerParams(vmem_limit_bytes=WIDE_LIMIT),
        cost_estimate=pl.CostEstimate(
            flops=2 * flops, bytes_accessed=TILES * keys * features * 2, transcendentals=TILES * keys * features
        ),
        name="attend",
    )(weight, query_t, *kv_tiles)


def far_gradients(group, query_t, weight, query_s, attended, probs, blocks, kv_tiles):
    _, count, width = blocks[0].shape
    features = query_s.shape[0]
    keys = kv_tiles[0].shape[0]
    flops = 2 * len(kv_tiles) * keys * features * HEAD_DIM
    partial = (2, len(group), count, 2 * HEAD_DIM)

    def kernel(*refs):
        far_kernel(group, *refs)

    return pl.pallas_call(
        kernel,
        out_shape=(
            jax.ShapeDtypeStruct(partial, F32),
            jax.ShapeDtypeStruct(partial, BF16),
            jax.ShapeDtypeStruct((HEAD_DIM, features), BF16),
            jax.ShapeDtypeStruct((features, HEAD_DIM), BF16),
            jax.ShapeDtypeStruct((8, features), F32),
            jax.ShapeDtypeStruct((HEAD_DIM, features), F32),
        ),
        in_specs=[VMEM_SPEC] * (6 + len(blocks) + len(kv_tiles)),
        out_specs=(VMEM_SPEC,) * 6,
        scratch_shapes=[
            pltpu.VMEM((keys, features), BF16),
            pltpu.VMEM((features, count), F32),
        ],
        compiler_params=PARAMS,
        cost_estimate=pl.CostEstimate(
            flops=4 * flops + 2 * weight.size * count, bytes_accessed=2 * weight.size, transcendentals=0
        ),
        name="far_gradients",
    )(query_t, weight, query_s, *attended, probs, *blocks, *kv_tiles)


def near_gradients(core, group, query_t, probs, shared, kv_tiles):
    features, _ = shared[1].shape
    keys = kv_tiles[0].shape[0]
    count = keys // 2
    n_kv = len(kv_tiles)
    flops = 2 * n_kv * keys * features * HEAD_DIM
    partial = (2, len(group), count, 2 * HEAD_DIM)
    result = ((HEAD_DIM, features), F32) if core == 1 else ((count, features), BF16)

    def kernel(*refs):
        near_kernel(core, group, *refs)

    return pl.pallas_call(
        kernel,
        out_shape=(
            jax.ShapeDtypeStruct(partial, BF16 if core == 1 else F32),
            jax.ShapeDtypeStruct(*result),
        ),
        in_specs=[VMEM_SPEC] * (7 + n_kv),
        out_specs=(VMEM_SPEC,) * 2,
        scratch_shapes=[pltpu.VMEM((keys, features), BF16), pltpu.VMEM((HEAD_DIM, features), F32)],
        compiler_params=PARAMS,
        cost_estimate=pl.CostEstimate(
            flops=4 * flops, bytes_accessed=2 * n_kv * keys * features, transcendentals=0
        ),
        name="near_gradients",
    )(query_t, probs, *shared, *kv_tiles)


def shards(queries, keys, values, out_grad, out_weight, seq_lengths, prompt_lengths):
    own, query_t, query_s = prepare(seq_lengths, prompt_lengths, keys, values, queries)
    own, out_grad = lax.optimization_barrier((own, out_grad))
    og_pair = jnp.stack([out_grad, head_swap(out_grad, 4)])
    reach = jnp.concatenate([ctx_swap(own, 8), ctx_swap(own, 12)], axis=0)
    pair = jnp.concatenate([own, ctx_swap(own, 2)], axis=0)
    across = head_swap(out_grad, 2)
    both = head_swap(across, 4)
    blocks = [og_pair, head_swap(og_pair, 1), head_swap(og_pair, 3), across, both]
    tiles = [*lax.optimization_barrier((pair, ctx_swap(pair, 4))), *lax.optimization_barrier((reach, ctx_swap(reach, 2)))]
    tiles += [ctx_swap(tile, 1) for tile in tiles]
    far, near = (2, 3), (0, 1)
    probs, *attended, weight = attend(out_weight, query_t, tiles)
    far_keep, far_send, grads_t, grads, delta, dquery_t = far_gradients(
        far, query_t, weight, query_s, attended, probs, blocks, [tiles[4 * core + n] for core in (1, 0) for n in far]
    )
    shared = (grads_t, grads, query_s, delta)
    near_send, dquery_t = near_gradients(1, near, query_t, probs, (*shared, dquery_t), [tiles[4 + n] for n in near])
    far_received, near_send = lax.optimization_barrier((ctx_swap(far_send, 1), near_send))
    far_sum = far_keep + far_received.astype(F32)
    far_payload = far_sum[1].astype(BF16)
    dquery_t, _ = lax.optimization_barrier((dquery_t, far_payload))
    near_keep, query_grad = near_gradients(0, near, query_t, probs, (*shared, dquery_t), [tiles[n] for n in near])
    near_sum = near_keep + ctx_swap(near_send, 1).astype(F32)
    far_across = ctx_swap(far_payload, 2)
    near_payload = near_sum[1].astype(BF16)
    far_across, _ = lax.optimization_barrier((far_across, near_payload))
    far_total = far_sum[0] + far_across.astype(F32)
    near_total = near_sum[0] + ctx_swap(near_payload, 2).astype(F32)
    beyond = lax.optimization_barrier((far_total[0].astype(BF16), far_total[1].astype(BF16)))
    near_total_own, beside = lax.optimization_barrier((near_total[0], near_total[1].astype(BF16)))
    received = [near_total_own, send_back(beyond[0], 8), send_back(beyond[1], 12), ctx_swap(beside, 4)]
    parts = [slice(0, HEAD_DIM), slice(HEAD_DIM, 2 * HEAD_DIM)]
    key_grad, value_grad = [sum(array[:, p].astype(F32) for array in received).astype(BF16) for p in parts]
    return (query_grad, key_grad, value_grad)


def solution(mesh):
    return jax.shard_map(
        shards,
        mesh=mesh,
        in_specs=(
            P("ctx", "head"),
            P("ctx", "head"),
            P("ctx", "head"),
            P("ctx", "head"),
            P("head", None),
            P(),
            P(),
        ),
        out_specs=(P("ctx", "head"), P("ctx", "head"), P("ctx", "head")),
        check_vma=False,
    )
```

```python
import math

import jax
import jax.numpy as jnp
from jax import lax
from jax.experimental import pallas as pl
from jax.experimental.pallas import tpu as pltpu
from jax.sharding import PartitionSpec as P

HEADS_Q = 40
HEADS_KV = 8
HEAD_DIM = 128
GROUP = HEADS_Q // HEADS_KV
HALF = 16
TILES = 8
NEG = -1e30
SCALE = 1.0 / math.sqrt(HEAD_DIM)
LOG2_SCALE = SCALE * math.log2(math.e)
BF16 = jnp.bfloat16
F32 = jnp.float32
VMEM_LIMIT = 32 * 1024 * 1024
WIDE_LIMIT = 40 * 1024 * 1024


def ctx_swap(value, bits):
    count = lax.axis_size("ctx")
    return lax.ppermute(value, "ctx", [(i, i ^ bits) for i in range(count)])


def send_back(value, bits):
    count = lax.axis_size("ctx")
    return lax.ppermute(value, "ctx", [(i, i ^ bits) for i in range(count) if i ^ bits < i])


def head_swap(value, bits):
    count = lax.axis_size("head")
    return lax.ppermute(value, "head", [(i, i ^ bits) for i in range(count)])


def dot_nn(a, b):
    return lax.dot_general(a, b, (((1,), (0,)), ((), ())), preferred_element_type=F32)


def dot_nt(a, b):
    return lax.dot_general(a, b, (((1,), (1,)), ((), ())), preferred_element_type=F32)


def heads(index):
    return slice(index * HEAD_DIM, (index + 1) * HEAD_DIM)


TILE_BLOCKS = (((0, 0), (1, 0)), ((0, 1), (1, 1)), ((0, 2), (0, 3)), ((1, 2), (1, 3)))


def tile_blocks(own, tile):
    return [own ^ (z * 4 + y * 2 + tile // 4) for y, z in TILE_BLOCKS[tile % 4]]


def own_geometry(qt_ref, count):
    geo = qt_ref[HEAD_DIM:, :count].astype(F32)
    place = lax.axis_index("ctx")
    own = place % HALF
    base = place - own
    low_block = jnp.maximum(jnp.min(geo[0:1]).astype(jnp.int32) - base, 0)
    return geo, place, own, base, low_block


def tile_active(own, low_block, tile):
    first, second = tile_blocks(own, tile)
    return ((first <= own) & (first >= low_block)) | ((second <= own) & (second >= low_block))


GEO_ROWS = 16
HEAD_RUNS = (slice(0, 256), slice(256, 512), slice(512, 640))


def fold_rows(values, reduce):
    rows, lanes = values.shape
    return reduce(values.reshape(rows // 8, 8, lanes), axis=0)


def prepare_kernel(lens_ref, prompts_ref, k_ref, v_ref, q_ref, kv_ref, qt_ref, qs_ref):
    kv_ref[:, :HEAD_DIM] = k_ref[...]
    kv_ref[:, HEAD_DIM:] = v_ref[...]
    for h in range(GROUP):
        qt_ref[:HEAD_DIM, heads(h)] = q_ref[:, heads(h)].T
        qs_ref[heads(h), :] = q_ref[:, heads(h)]
    rows, count = GEO_ROWS, q_ref.shape[0]
    position = lax.axis_index("ctx") * count + lax.broadcasted_iota(jnp.int32, (rows, count), 1)
    start = jnp.int32(0)
    begin = jnp.zeros((rows, count), jnp.int32)
    answer_from = jnp.zeros((rows, count), jnp.int32)
    for s in range(lens_ref.shape[0]):
        answer = start + jnp.minimum(prompts_ref[s], lens_ref[s] - 1)
        begin = jnp.where(position >= start, start, begin)
        answer_from = jnp.where(position >= start, answer, answer_from)
        start = start + lens_ref[s]
    kind = lax.broadcasted_iota(jnp.int32, (rows, count), 0)
    answer = jnp.where(position >= answer_from, 1, 0)
    small = jnp.where(kind == 0, begin // count, jnp.where(kind == 1, begin % count, answer))
    qt_ref[HEAD_DIM:, :count] = small.astype(F32).astype(BF16)
    qt_ref[HEAD_DIM:, count:] = jnp.zeros((rows, qt_ref.shape[1] - count), BF16)


def attend_kernel(w_ref, qt_ref, *refs):
    kv_refs = refs[:TILES]
    p_ref, o_ref, inv_ref, w_out, s_ref, m_ref, l_ref, sem = refs[TILES:]
    weights = pltpu.make_async_copy(w_ref, w_out, sem)
    weights.start()
    count = kv_refs[0].shape[0] // 2
    geo, place, own, base, low_block = own_geometry(qt_ref, count)
    q_pos = place * count + lax.broadcasted_iota(jnp.int32, (count, count), 1)
    q_start = (geo[0:1] * count + geo[1:2]).astype(jnp.int32)
    m_ref[...] = jnp.full(m_ref.shape, NEG, F32)
    l_ref[...] = jnp.zeros(l_ref.shape, F32)
    o_ref[...] = jnp.zeros(o_ref.shape, F32)

    for tile in range(TILES):

        @pl.when(tile_active(own, low_block, tile))
        def _(tile=tile):
            for n, block in enumerate(tile_blocks(own, tile)):
                rows = slice(n * count, (n + 1) * count)
                k_pos = (base + block) * count + lax.broadcasted_iota(jnp.int32, (count, count), 0)
                bias = jnp.where((k_pos <= q_pos) & (k_pos >= q_start), 0.0, NEG).astype(F32)
                keys = kv_refs[tile][rows, :HEAD_DIM]
                for run in HEAD_RUNS:
                    wide = (run.stop - run.start) // HEAD_DIM
                    scores = dot_nn(keys, qt_ref[:HEAD_DIM, run]) * LOG2_SCALE + jnp.concatenate([bias] * wide, axis=1)
                    s_ref[tile, rows, run] = scores
                    m_ref[:, run] = jnp.maximum(m_ref[:, run], fold_rows(scores, jnp.max))

    m_ref[...] = jnp.broadcast_to(jnp.max(m_ref[...], axis=0, keepdims=True), m_ref.shape)

    for tile in range(TILES):

        @pl.when(tile_active(own, low_block, tile))
        def _(tile=tile):
            values = kv_refs[tile][:, HEAD_DIM:].T
            for run in HEAD_RUNS:
                for n in range(2):
                    rows = slice(n * count, (n + 1) * count)
                    probs = jnp.exp2(s_ref[tile, rows, run] - m_ref[0:1, run])
                    l_ref[:, run] = l_ref[:, run] + fold_rows(probs, jnp.sum)
                    p_ref[tile, rows, run] = probs.astype(BF16)
                o_ref[:, run] += dot_nn(values, p_ref[tile, :, run])

    inverse = 1.0 / jnp.sum(l_ref[...], axis=0, keepdims=True)
    inv_ref[...] = jnp.broadcast_to(inverse, inv_ref.shape)
    weights.wait()


def tile_gradients(tile, p_ref, kv_ref, gt_ref, g_ref, qs_ref, delta_ref, ds_ref, dqt_ref, out):
    count = out.shape[2]
    keys, values = kv_ref[:, :HEAD_DIM], kv_ref[:, HEAD_DIM:]
    for run in HEAD_RUNS:
        for n in range(2):
            rows = slice(n * count, (n + 1) * count)
            dprobs = dot_nn(values[rows], gt_ref[:, run])
            probs = p_ref[tile, rows, run].astype(F32)
            ds_ref[rows, run] = (probs * (dprobs - delta_ref[0:1, run])).astype(BF16)
    dvalue = dot_nn(p_ref[tile], g_ref[...])
    dkey = dot_nn(ds_ref[...], qs_ref[...]) * SCALE
    dqt_ref[...] += dot_nn(keys.T, ds_ref[...])
    for n, (y, z) in enumerate(TILE_BLOCKS[tile % 4]):
        rows = slice(n * count, (n + 1) * count)
        out[y, z % 2, :, :HEAD_DIM] = dkey[rows].astype(out.dtype)
        out[y, z % 2, :, HEAD_DIM:] = dvalue[rows].astype(out.dtype)


def all_tiles(outs, group, qt_ref, count, p_ref, kv_refs, gt_ref, g_ref, qs_ref, delta_ref, ds_ref, dqt_ref):
    _, _, own, _, low_block = own_geometry(qt_ref, count)
    for n_core, (core, out) in enumerate(outs):
        for n, member in enumerate(group):
            tile = core * 4 + member
            kv_ref = kv_refs[n_core * len(group) + n]
            active = tile_active(own, low_block, tile)

            @pl.when(active)
            def _(tile=tile, kv_ref=kv_ref, out=out):
                tile_gradients(tile, p_ref, kv_ref, gt_ref, g_ref, qs_ref, delta_ref, ds_ref, dqt_ref, out)

            @pl.when(jnp.logical_not(active))
            def _(tile=tile, out=out):
                for y, z in TILE_BLOCKS[tile % 4]:
                    out[y, z % 2] = jnp.zeros(out.shape[2:], out.dtype)


def add_parts(acc_ref, total, w_ref, parts):
    mine = lax.axis_index("head")
    for slot, block in parts:
        width = block.shape[1]
        columns = pl.ds(pl.multiple_of((mine ^ slot) * width, HEAD_DIM), width)
        part = dot_nt(w_ref[:, columns], block)
        acc_ref[...] = part if total is None else total + part
        total = acc_ref[...]


def project_kernel(w_ref, pair_ref, one_ref, three_ref, across_ref, acc_ref):
    parts = [(0, pair_ref[0]), (4, pair_ref[1]), (2, across_ref[...]), (1, one_ref[0])]
    parts += [(5, one_ref[1]), (3, three_ref[0]), (7, three_ref[1])]
    add_parts(acc_ref, None, w_ref, parts)


def far_kernel(group, qt_ref, w_ref, acc_in, og_ref, qs_ref, o_ref, inv_ref, p_ref, *refs):
    kv_refs = refs[: 2 * len(group)]
    keep_ref, send_ref, gt_ref, g_ref, delta_ref, dqt_ref, ds_ref, acc_ref = refs[2 * len(group) :]
    count = og_ref.shape[0]
    add_parts(acc_ref, acc_in[...], w_ref, [(6, og_ref[...])])
    answer = qt_ref[HEAD_DIM:, :count].astype(F32)[2:3]
    for h in range(GROUP):
        inverse = inv_ref[0:1, heads(h)]
        grads = (acc_ref[heads(h), :] * answer).astype(BF16).astype(F32)
        scaled = (grads * inverse).astype(BF16)
        gt_ref[:, heads(h)] = scaled
        g_ref[heads(h), :] = scaled.T
        delta = jnp.sum(scaled.astype(F32) * (o_ref[:, heads(h)] * inverse), axis=0, keepdims=True)
        delta_ref[:, heads(h)] = jnp.broadcast_to(delta, (8, HEAD_DIM))
    dqt_ref[...] = jnp.zeros(dqt_ref.shape, F32)
    outs = ((1, send_ref), (0, keep_ref))
    all_tiles(outs, group, qt_ref, count, p_ref, kv_refs, gt_ref, g_ref, qs_ref, delta_ref, ds_ref, dqt_ref)


def near_kernel(core, group, qt_ref, p_ref, gt_ref, g_ref, qs_ref, delta_ref, dqt_in, *refs):
    kv_refs = refs[: len(group)]
    out_ref, result_ref, ds_ref, dqt_ref = refs[len(group) :]
    count = out_ref.shape[2]
    dqt_ref[...] = dqt_in[...]
    all_tiles(((core, out_ref),), group, qt_ref, count, p_ref, kv_refs, gt_ref, g_ref, qs_ref, delta_ref, ds_ref, dqt_ref)
    if core == 1:
        result_ref[...] = dqt_ref[...]
    else:
        for h in range(GROUP):
            result_ref[:, heads(h)] = (dqt_ref[:, heads(h)] * SCALE).T.astype(BF16)


VMEM_SPEC = pl.BlockSpec(memory_space=pltpu.VMEM)
SMEM_SPEC = pl.BlockSpec(memory_space=pltpu.SMEM)
ANY_SPEC = pl.BlockSpec(memory_space=pltpu.HBM)
PARAMS = pltpu.CompilerParams(vmem_limit_bytes=VMEM_LIMIT)


def prepare(seq_lengths, prompt_lengths, keys, values, queries):
    count, features = queries.shape
    return pl.pallas_call(
        prepare_kernel,
        out_shape=(
            jax.ShapeDtypeStruct((count, 2 * HEAD_DIM), BF16),
            jax.ShapeDtypeStruct((HEAD_DIM + GEO_ROWS, features), BF16),
            jax.ShapeDtypeStruct((features, HEAD_DIM), BF16),
        ),
        in_specs=[SMEM_SPEC] * 2 + [VMEM_SPEC] * 3,
        out_specs=(VMEM_SPEC,) * 3,
        name="prepare",
    )(seq_lengths, prompt_lengths, keys, values, queries)


def attend(weight, query_t, kv_tiles):
    _, features = query_t.shape
    keys = kv_tiles[0].shape[0]
    flops = 2 * TILES * keys * features * HEAD_DIM
    return pl.pallas_call(
        attend_kernel,
        out_shape=(
            jax.ShapeDtypeStruct((TILES, keys, features), BF16),
            jax.ShapeDtypeStruct((HEAD_DIM, features), F32),
            jax.ShapeDtypeStruct((8, features), F32),
            jax.ShapeDtypeStruct(weight.shape, BF16),
        ),
        in_specs=[ANY_SPEC] + [VMEM_SPEC] * (1 + TILES),
        out_specs=(VMEM_SPEC,) * 4,
        scratch_shapes=[
            pltpu.VMEM((TILES, keys, features), F32),
            pltpu.VMEM((8, features), F32),
            pltpu.VMEM((8, features), F32),
            pltpu.SemaphoreType.DMA,
        ],
        compiler_params=pltpu.CompilerParams(vmem_limit_bytes=WIDE_LIMIT),
        cost_estimate=pl.CostEstimate(
            flops=2 * flops, bytes_accessed=TILES * keys * features * 2, transcendentals=TILES * keys * features
        ),
        name="attend",
    )(weight, query_t, *kv_tiles)


def project(weight, pair, one, three, across):
    count, _ = across.shape
    features = weight.shape[0]
    return pl.pallas_call(
        project_kernel,
        out_shape=jax.ShapeDtypeStruct((features, count), F32),
        in_specs=[VMEM_SPEC] * 5,
        out_specs=VMEM_SPEC,
        compiler_params=PARAMS,
        cost_estimate=pl.CostEstimate(flops=2 * weight.size * count, bytes_accessed=2 * weight.size, transcendentals=0),
        name="project",
    )(weight, pair, one, three, across)


def far_gradients(group, query_t, weight, acc, last, query_s, attended, probs, kv_tiles):
    count, _ = last.shape
    features = query_s.shape[0]
    keys = kv_tiles[0].shape[0]
    flops = 2 * len(kv_tiles) * keys * features * HEAD_DIM
    partial = (2, len(group), count, 2 * HEAD_DIM)

    def kernel(*refs):
        far_kernel(group, *refs)

    return pl.pallas_call(
        kernel,
        out_shape=(
            jax.ShapeDtypeStruct(partial, F32),
            jax.ShapeDtypeStruct(partial, BF16),
            jax.ShapeDtypeStruct((HEAD_DIM, features), BF16),
            jax.ShapeDtypeStruct((features, HEAD_DIM), BF16),
            jax.ShapeDtypeStruct((8, features), F32),
            jax.ShapeDtypeStruct((HEAD_DIM, features), F32),
        ),
        in_specs=[VMEM_SPEC] * (8 + len(kv_tiles)),
        out_specs=(VMEM_SPEC,) * 6,
        scratch_shapes=[
            pltpu.VMEM((keys, features), BF16),
            pltpu.VMEM((features, count), F32),
        ],
        compiler_params=PARAMS,
        cost_estimate=pl.CostEstimate(
            flops=4 * flops + 2 * weight.size * count, bytes_accessed=2 * weight.size, transcendentals=0
        ),
        name="far_gradients",
    )(query_t, weight, acc, last, query_s, *attended, probs, *kv_tiles)


def near_gradients(core, group, query_t, probs, shared, kv_tiles):
    features, _ = shared[1].shape
    keys = kv_tiles[0].shape[0]
    count = keys // 2
    n_kv = len(kv_tiles)
    flops = 2 * n_kv * keys * features * HEAD_DIM
    partial = (2, len(group), count, 2 * HEAD_DIM)
    result = ((HEAD_DIM, features), F32) if core == 1 else ((count, features), BF16)

    def kernel(*refs):
        near_kernel(core, group, *refs)

    return pl.pallas_call(
        kernel,
        out_shape=(
            jax.ShapeDtypeStruct(partial, BF16 if core == 1 else F32),
            jax.ShapeDtypeStruct(*result),
        ),
        in_specs=[VMEM_SPEC] * (7 + n_kv),
        out_specs=(VMEM_SPEC,) * 2,
        scratch_shapes=[pltpu.VMEM((keys, features), BF16), pltpu.VMEM((HEAD_DIM, features), F32)],
        compiler_params=PARAMS,
        cost_estimate=pl.CostEstimate(
            flops=4 * flops, bytes_accessed=2 * n_kv * keys * features, transcendentals=0
        ),
        name="near_gradients",
    )(query_t, probs, *shared, *kv_tiles)


def shards(queries, keys, values, out_grad, out_weight, seq_lengths, prompt_lengths):
    own, query_t, query_s = prepare(seq_lengths, prompt_lengths, keys, values, queries)
    own, out_grad = lax.optimization_barrier((own, out_grad))
    og_pair = jnp.stack([out_grad, head_swap(out_grad, 4)])
    reach = jnp.concatenate([ctx_swap(own, 8), ctx_swap(own, 12)], axis=0)
    pair = jnp.concatenate([own, ctx_swap(own, 2)], axis=0)
    across = head_swap(out_grad, 2)
    both = head_swap(across, 4)
    one, three = head_swap(og_pair, 1), head_swap(og_pair, 3)
    tiles = [*lax.optimization_barrier((pair, ctx_swap(pair, 4))), *lax.optimization_barrier((reach, ctx_swap(reach, 2)))]
    tiles += [ctx_swap(tile, 1) for tile in tiles]
    far, near = (2, 3), (0, 1)
    probs, *attended, weight = attend(out_weight, query_t, tiles)
    acc = project(weight, og_pair, one, three, across)
    far_keep, far_send, grads_t, grads, delta, dquery_t = far_gradients(
        far, query_t, weight, acc, both, query_s, attended, probs, [tiles[4 * core + n] for core in (1, 0) for n in far]
    )
    shared = (grads_t, grads, query_s, delta)
    near_send, dquery_t = near_gradients(1, near, query_t, probs, (*shared, dquery_t), [tiles[4 + n] for n in near])
    far_received, near_send = lax.optimization_barrier((ctx_swap(far_send, 1), near_send))
    far_sum = far_keep + far_received.astype(F32)
    far_payload = far_sum[1].astype(BF16)
    dquery_t, _ = lax.optimization_barrier((dquery_t, far_payload))
    near_keep, query_grad = near_gradients(0, near, query_t, probs, (*shared, dquery_t), [tiles[n] for n in near])
    near_sum = near_keep + ctx_swap(near_send, 1).astype(F32)
    far_across = ctx_swap(far_payload, 2)
    near_payload = near_sum[1].astype(BF16)
    far_across, _ = lax.optimization_barrier((far_across, near_payload))
    far_total = far_sum[0] + far_across.astype(F32)
    near_total = near_sum[0] + ctx_swap(near_payload, 2).astype(F32)
    beyond = lax.optimization_barrier((far_total[0].astype(BF16), far_total[1].astype(BF16)))
    near_total_own, beside = lax.optimization_barrier((near_total[0], near_total[1].astype(BF16)))
    received = [near_total_own, send_back(beyond[0], 8), send_back(beyond[1], 12), ctx_swap(beside, 4)]
    parts = [slice(0, HEAD_DIM), slice(HEAD_DIM, 2 * HEAD_DIM)]
    key_grad, value_grad = [sum(array[:, p].astype(F32) for array in received).astype(BF16) for p in parts]
    return (query_grad, key_grad, value_grad)


def solution(mesh):
    return jax.shard_map(
        shards,
        mesh=mesh,
        in_specs=(
            P("ctx", "head"),
            P("ctx", "head"),
            P("ctx", "head"),
            P("ctx", "head"),
            P("head", None),
            P(),
            P(),
        ),
        out_specs=(P("ctx", "head"), P("ctx", "head"), P("ctx", "head")),
        check_vma=False,
    )
```

```python
import math

import jax
import jax.numpy as jnp
from jax import lax
from jax.experimental import pallas as pl
from jax.experimental.pallas import tpu as pltpu
from jax.sharding import PartitionSpec as P

HEADS_Q = 40
HEADS_KV = 8
HEAD_DIM = 128
GROUP = HEADS_Q // HEADS_KV
HALF = 16
TILES = 8
NEG = -1e30
SCALE = 1.0 / math.sqrt(HEAD_DIM)
LOG2_SCALE = SCALE * math.log2(math.e)
BF16 = jnp.bfloat16
F32 = jnp.float32
VMEM_LIMIT = 32 * 1024 * 1024
WIDE_LIMIT = 40 * 1024 * 1024


def ctx_swap(value, bits):
    count = lax.axis_size("ctx")
    return lax.ppermute(value, "ctx", [(i, i ^ bits) for i in range(count)])


def send_back(value, bits):
    count = lax.axis_size("ctx")
    return lax.ppermute(value, "ctx", [(i, i ^ bits) for i in range(count) if i ^ bits < i])


def head_swap(value, bits):
    count = lax.axis_size("head")
    return lax.ppermute(value, "head", [(i, i ^ bits) for i in range(count)])


def dot_nn(a, b):
    return lax.dot_general(a, b, (((1,), (0,)), ((), ())), preferred_element_type=F32)


def dot_nt(a, b):
    return lax.dot_general(a, b, (((1,), (1,)), ((), ())), preferred_element_type=F32)


def heads(index):
    return slice(index * HEAD_DIM, (index + 1) * HEAD_DIM)


TILE_BLOCKS = (((0, 0), (1, 0)), ((0, 1), (1, 1)), ((0, 2), (0, 3)), ((1, 2), (1, 3)))


def tile_blocks(own, tile):
    return [own ^ (z * 4 + y * 2 + tile // 4) for y, z in TILE_BLOCKS[tile % 4]]


def own_geometry(qt_ref, count):
    geo = qt_ref[HEAD_DIM:, :count].astype(F32)
    place = lax.axis_index("ctx")
    own = place % HALF
    base = place - own
    low_block = jnp.maximum(jnp.min(geo[0:1]).astype(jnp.int32) - base, 0)
    return geo, place, own, base, low_block


def tile_active(own, low_block, tile):
    first, second = tile_blocks(own, tile)
    return ((first <= own) & (first >= low_block)) | ((second <= own) & (second >= low_block))


GEO_ROWS = 16
HEAD_RUNS = (slice(0, 256), slice(256, 512), slice(512, 640))


def fold_rows(values, reduce):
    rows, lanes = values.shape
    return reduce(values.reshape(rows // 8, 8, lanes), axis=0)


def prepare_kernel(lens_ref, prompts_ref, k_ref, v_ref, q_ref, kv_ref, qt_ref, qs_ref):
    kv_ref[:, :HEAD_DIM] = k_ref[...]
    kv_ref[:, HEAD_DIM:] = v_ref[...]
    for h in range(GROUP):
        qt_ref[:HEAD_DIM, heads(h)] = q_ref[:, heads(h)].T
        qs_ref[heads(h), :] = q_ref[:, heads(h)]
    rows, count = GEO_ROWS, q_ref.shape[0]
    position = lax.axis_index("ctx") * count + lax.broadcasted_iota(jnp.int32, (rows, count), 1)
    start = jnp.int32(0)
    begin = jnp.zeros((rows, count), jnp.int32)
    answer_from = jnp.zeros((rows, count), jnp.int32)
    for s in range(lens_ref.shape[0]):
        answer = start + jnp.minimum(prompts_ref[s], lens_ref[s] - 1)
        begin = jnp.where(position >= start, start, begin)
        answer_from = jnp.where(position >= start, answer, answer_from)
        start = start + lens_ref[s]
    kind = lax.broadcasted_iota(jnp.int32, (rows, count), 0)
    answer = jnp.where(position >= answer_from, 1, 0)
    small = jnp.where(kind == 0, begin // count, jnp.where(kind == 1, begin % count, answer))
    qt_ref[HEAD_DIM:, :count] = small.astype(F32).astype(BF16)
    qt_ref[HEAD_DIM:, count:] = jnp.zeros((rows, qt_ref.shape[1] - count), BF16)


def attend_kernel(w_ref, qt_ref, *refs):
    kv_refs = refs[:TILES]
    p_ref, o_ref, inv_ref, w_out, s_ref, m_ref, l_ref, sem = refs[TILES:]
    weights = pltpu.make_async_copy(w_ref, w_out, sem)
    weights.start()
    count = kv_refs[0].shape[0] // 2
    geo, place, own, base, low_block = own_geometry(qt_ref, count)
    q_pos = place * count + lax.broadcasted_iota(jnp.int32, (count, count), 1)
    q_start = (geo[0:1] * count + geo[1:2]).astype(jnp.int32)
    m_ref[...] = jnp.full(m_ref.shape, NEG, F32)
    l_ref[...] = jnp.zeros(l_ref.shape, F32)
    o_ref[...] = jnp.zeros(o_ref.shape, F32)

    for tile in range(TILES):

        @pl.when(tile_active(own, low_block, tile))
        def _(tile=tile):
            for n, block in enumerate(tile_blocks(own, tile)):
                rows = slice(n * count, (n + 1) * count)
                k_pos = (base + block) * count + lax.broadcasted_iota(jnp.int32, (count, count), 0)
                bias = jnp.where((k_pos <= q_pos) & (k_pos >= q_start), 0.0, NEG).astype(F32)
                keys = kv_refs[tile][rows, :HEAD_DIM]
                for run in HEAD_RUNS:
                    wide = (run.stop - run.start) // HEAD_DIM
                    scores = dot_nn(keys, qt_ref[:HEAD_DIM, run]) * LOG2_SCALE + jnp.concatenate([bias] * wide, axis=1)
                    s_ref[tile, rows, run] = scores
                    m_ref[:, run] = jnp.maximum(m_ref[:, run], fold_rows(scores, jnp.max))

    m_ref[...] = jnp.broadcast_to(jnp.max(m_ref[...], axis=0, keepdims=True), m_ref.shape)

    for tile in range(TILES):

        @pl.when(tile_active(own, low_block, tile))
        def _(tile=tile):
            values = kv_refs[tile][:, HEAD_DIM:].T
            for run in HEAD_RUNS:
                for n in range(2):
                    rows = slice(n * count, (n + 1) * count)
                    probs = jnp.exp2(s_ref[tile, rows, run] - m_ref[0:1, run])
                    l_ref[:, run] = l_ref[:, run] + fold_rows(probs, jnp.sum)
                    p_ref[tile, rows, run] = probs.astype(BF16)
                o_ref[:, run] += dot_nn(values, p_ref[tile, :, run])

    inverse = 1.0 / jnp.sum(l_ref[...], axis=0, keepdims=True)
    inv_ref[...] = jnp.broadcast_to(inverse, inv_ref.shape)
    weights.wait()


def tile_gradients(tile, p_ref, kv_ref, gt_ref, g_ref, qs_ref, delta_ref, ds_ref, dqt_ref, out):
    count = out.shape[2]
    keys, values = kv_ref[:, :HEAD_DIM], kv_ref[:, HEAD_DIM:]
    for run in HEAD_RUNS:
        for n in range(2):
            rows = slice(n * count, (n + 1) * count)
            dprobs = dot_nn(values[rows], gt_ref[:, run])
            probs = p_ref[tile, rows, run].astype(F32)
            ds_ref[rows, run] = (probs * (dprobs - delta_ref[0:1, run])).astype(BF16)
    dvalue = dot_nn(p_ref[tile], g_ref[...])
    dkey = dot_nn(ds_ref[...], qs_ref[...]) * SCALE
    dqt_ref[...] += dot_nn(keys.T, ds_ref[...])
    for n, (y, z) in enumerate(TILE_BLOCKS[tile % 4]):
        rows = slice(n * count, (n + 1) * count)
        out[y, z % 2, :, :HEAD_DIM] = dkey[rows].astype(out.dtype)
        out[y, z % 2, :, HEAD_DIM:] = dvalue[rows].astype(out.dtype)


def all_tiles(outs, group, qt_ref, count, p_ref, kv_refs, gt_ref, g_ref, qs_ref, delta_ref, ds_ref, dqt_ref):
    _, _, own, _, low_block = own_geometry(qt_ref, count)
    for n_core, (core, out) in enumerate(outs):
        for n, member in enumerate(group):
            tile = core * 4 + member
            kv_ref = kv_refs[n_core * len(group) + n]
            active = tile_active(own, low_block, tile)

            @pl.when(active)
            def _(tile=tile, kv_ref=kv_ref, out=out):
                tile_gradients(tile, p_ref, kv_ref, gt_ref, g_ref, qs_ref, delta_ref, ds_ref, dqt_ref, out)

            @pl.when(jnp.logical_not(active))
            def _(tile=tile, out=out):
                for y, z in TILE_BLOCKS[tile % 4]:
                    out[y, z % 2] = jnp.zeros(out.shape[2:], out.dtype)


def add_parts(acc_ref, total, w_ref, parts):
    mine = lax.axis_index("head")
    for slot, block in parts:
        width = block.shape[1]
        columns = pl.ds(pl.multiple_of((mine ^ slot) * width, HEAD_DIM), width)
        part = dot_nt(w_ref[:, columns], block)
        acc_ref[...] = part if total is None else total + part
        total = acc_ref[...]


def project_kernel(w_ref, pair_ref, one_ref, three_ref, across_ref, acc_ref):
    parts = [(0, pair_ref[0]), (4, pair_ref[1]), (2, across_ref[...]), (1, one_ref[0])]
    parts += [(5, one_ref[1]), (3, three_ref[0]), (7, three_ref[1])]
    add_parts(acc_ref, None, w_ref, parts)


def far_kernel(group, qt_ref, w_ref, acc_in, og_ref, qs_ref, o_ref, inv_ref, p_ref, *refs):
    kv_refs = refs[: 2 * len(group)]
    keep_ref, send_ref, gt_ref, g_ref, delta_ref, dqt_ref, ds_ref, acc_ref = refs[2 * len(group) :]
    count = og_ref.shape[0]
    add_parts(acc_ref, acc_in[...], w_ref, [(6, og_ref[...])])
    answer = qt_ref[HEAD_DIM:, :count].astype(F32)[2:3]
    for h in range(GROUP):
        inverse = inv_ref[0:1, heads(h)]
        grads = (acc_ref[heads(h), :] * answer).astype(BF16).astype(F32)
        scaled = (grads * inverse).astype(BF16)
        gt_ref[:, heads(h)] = scaled
        g_ref[heads(h), :] = scaled.T
        delta = jnp.sum(scaled.astype(F32) * (o_ref[:, heads(h)] * inverse), axis=0, keepdims=True)
        delta_ref[:, heads(h)] = jnp.broadcast_to(delta, (8, HEAD_DIM))
    dqt_ref[...] = jnp.zeros(dqt_ref.shape, F32)
    outs = ((1, send_ref), (0, keep_ref))
    all_tiles(outs, group, qt_ref, count, p_ref, kv_refs, gt_ref, g_ref, qs_ref, delta_ref, ds_ref, dqt_ref)


def near_kernel(core, group, qt_ref, p_ref, gt_ref, g_ref, qs_ref, delta_ref, dqt_in, *refs):
    kv_refs = refs[: len(group)]
    out_ref, result_ref, ds_ref, dqt_ref = refs[len(group) :]
    count = out_ref.shape[2]
    dqt_ref[...] = dqt_in[...]
    all_tiles(((core, out_ref),), group, qt_ref, count, p_ref, kv_refs, gt_ref, g_ref, qs_ref, delta_ref, ds_ref, dqt_ref)
    if core == 1:
        result_ref[...] = dqt_ref[...]
    else:
        for h in range(GROUP):
            result_ref[:, heads(h)] = (dqt_ref[:, heads(h)] * SCALE).T.astype(BF16)


VMEM_SPEC = pl.BlockSpec(memory_space=pltpu.VMEM)
SMEM_SPEC = pl.BlockSpec(memory_space=pltpu.SMEM)
ANY_SPEC = pl.BlockSpec(memory_space=pltpu.HBM)
PARAMS = pltpu.CompilerParams(vmem_limit_bytes=VMEM_LIMIT)


def prepare(seq_lengths, prompt_lengths, keys, values, queries):
    count, features = queries.shape
    return pl.pallas_call(
        prepare_kernel,
        out_shape=(
            jax.ShapeDtypeStruct((count, 2 * HEAD_DIM), BF16),
            jax.ShapeDtypeStruct((HEAD_DIM + GEO_ROWS, features), BF16),
            jax.ShapeDtypeStruct((features, HEAD_DIM), BF16),
        ),
        in_specs=[SMEM_SPEC] * 2 + [VMEM_SPEC] * 3,
        out_specs=(VMEM_SPEC,) * 3,
        name="prepare",
    )(seq_lengths, prompt_lengths, keys, values, queries)


def attend(weight, query_t, kv_tiles):
    _, features = query_t.shape
    keys = kv_tiles[0].shape[0]
    flops = 2 * TILES * keys * features * HEAD_DIM
    return pl.pallas_call(
        attend_kernel,
        out_shape=(
            jax.ShapeDtypeStruct((TILES, keys, features), BF16),
            jax.ShapeDtypeStruct((HEAD_DIM, features), F32),
            jax.ShapeDtypeStruct((8, features), F32),
            jax.ShapeDtypeStruct(weight.shape, BF16),
        ),
        in_specs=[ANY_SPEC] + [VMEM_SPEC] * (1 + TILES),
        out_specs=(VMEM_SPEC,) * 4,
        scratch_shapes=[
            pltpu.VMEM((TILES, keys, features), F32),
            pltpu.VMEM((8, features), F32),
            pltpu.VMEM((8, features), F32),
            pltpu.SemaphoreType.DMA,
        ],
        compiler_params=pltpu.CompilerParams(vmem_limit_bytes=WIDE_LIMIT),
        cost_estimate=pl.CostEstimate(
            flops=2 * flops, bytes_accessed=TILES * keys * features * 2, transcendentals=TILES * keys * features
        ),
        name="attend",
    )(weight, query_t, *kv_tiles)


def project(weight, pair, one, three, across):
    count, _ = across.shape
    features = weight.shape[0]
    return pl.pallas_call(
        project_kernel,
        out_shape=jax.ShapeDtypeStruct((features, count), F32),
        in_specs=[VMEM_SPEC] * 5,
        out_specs=VMEM_SPEC,
        compiler_params=PARAMS,
        cost_estimate=pl.CostEstimate(flops=2 * weight.size * count, bytes_accessed=2 * weight.size, transcendentals=0),
        name="project",
    )(weight, pair, one, three, across)


def far_gradients(group, query_t, weight, acc, last, query_s, attended, probs, kv_tiles):
    count, _ = last.shape
    features = query_s.shape[0]
    keys = kv_tiles[0].shape[0]
    flops = 2 * len(kv_tiles) * keys * features * HEAD_DIM
    partial = (2, len(group), count, 2 * HEAD_DIM)

    def kernel(*refs):
        far_kernel(group, *refs)

    return pl.pallas_call(
        kernel,
        out_shape=(
            jax.ShapeDtypeStruct(partial, F32),
            jax.ShapeDtypeStruct(partial, BF16),
            jax.ShapeDtypeStruct((HEAD_DIM, features), BF16),
            jax.ShapeDtypeStruct((features, HEAD_DIM), BF16),
            jax.ShapeDtypeStruct((8, features), F32),
            jax.ShapeDtypeStruct((HEAD_DIM, features), F32),
        ),
        in_specs=[VMEM_SPEC] * (8 + len(kv_tiles)),
        out_specs=(VMEM_SPEC,) * 6,
        scratch_shapes=[
            pltpu.VMEM((keys, features), BF16),
            pltpu.VMEM((features, count), F32),
        ],
        compiler_params=PARAMS,
        cost_estimate=pl.CostEstimate(
            flops=4 * flops + 2 * weight.size * count, bytes_accessed=2 * weight.size, transcendentals=0
        ),
        name="far_gradients",
    )(query_t, weight, acc, last, query_s, *attended, probs, *kv_tiles)


def near_gradients(core, group, query_t, probs, shared, kv_tiles):
    features, _ = shared[1].shape
    keys = kv_tiles[0].shape[0]
    count = keys // 2
    n_kv = len(kv_tiles)
    flops = 2 * n_kv * keys * features * HEAD_DIM
    partial = (2, len(group), count, 2 * HEAD_DIM)
    result = ((HEAD_DIM, features), F32) if core == 1 else ((count, features), BF16)

    def kernel(*refs):
        near_kernel(core, group, *refs)

    return pl.pallas_call(
        kernel,
        out_shape=(
            jax.ShapeDtypeStruct(partial, BF16 if core == 1 else F32),
            jax.ShapeDtypeStruct(*result),
        ),
        in_specs=[VMEM_SPEC] * (7 + n_kv),
        out_specs=(VMEM_SPEC,) * 2,
        scratch_shapes=[pltpu.VMEM((keys, features), BF16), pltpu.VMEM((HEAD_DIM, features), F32)],
        compiler_params=PARAMS,
        cost_estimate=pl.CostEstimate(
            flops=4 * flops, bytes_accessed=2 * n_kv * keys * features, transcendentals=0
        ),
        name="near_gradients",
    )(query_t, probs, *shared, *kv_tiles)


def shards(queries, keys, values, out_grad, out_weight, seq_lengths, prompt_lengths):
    own, query_t, query_s = prepare(seq_lengths, prompt_lengths, keys, values, queries)
    own, out_grad = lax.optimization_barrier((own, out_grad))
    og_pair = jnp.stack([out_grad, head_swap(out_grad, 4)])
    reach = jnp.concatenate([ctx_swap(own, 8), ctx_swap(own, 12)], axis=0)
    mate = ctx_swap(own, 2)
    pair = jnp.concatenate([own, mate], axis=0)
    later, _ = lax.optimization_barrier((out_grad, mate))
    across = head_swap(later, 2)
    both = head_swap(across, 4)
    one, three = head_swap(og_pair, 1), head_swap(og_pair, 3)
    tiles = [*lax.optimization_barrier((pair, ctx_swap(pair, 4))), *lax.optimization_barrier((reach, ctx_swap(reach, 2)))]
    tiles += [ctx_swap(tile, 1) for tile in tiles]
    far, near = (2, 3), (0, 1)
    probs, *attended, weight = attend(out_weight, query_t, tiles)
    acc = project(weight, og_pair, one, three, across)
    far_keep, far_send, grads_t, grads, delta, dquery_t = far_gradients(
        far, query_t, weight, acc, both, query_s, attended, probs, [tiles[4 * core + n] for core in (1, 0) for n in far]
    )
    shared = (grads_t, grads, query_s, delta)
    near_send, dquery_t = near_gradients(1, near, query_t, probs, (*shared, dquery_t), [tiles[4 + n] for n in near])
    far_received, near_send = lax.optimization_barrier((ctx_swap(far_send, 1), near_send))
    far_sum = far_keep + far_received.astype(F32)
    far_payload = far_sum[1].astype(BF16)
    dquery_t, _ = lax.optimization_barrier((dquery_t, far_payload))
    near_keep, query_grad = near_gradients(0, near, query_t, probs, (*shared, dquery_t), [tiles[n] for n in near])
    near_sum = near_keep + ctx_swap(near_send, 1).astype(F32)
    far_across = ctx_swap(far_payload, 2)
    near_payload = near_sum[1].astype(BF16)
    far_across, _ = lax.optimization_barrier((far_across, near_payload))
    far_total = far_sum[0] + far_across.astype(F32)
    near_total = near_sum[0] + ctx_swap(near_payload, 2).astype(F32)
    beyond = lax.optimization_barrier((far_total[0].astype(BF16), far_total[1].astype(BF16)))
    near_total_own, beside = lax.optimization_barrier((near_total[0], near_total[1].astype(BF16)))
    received = [near_total_own, send_back(beyond[0], 8), send_back(beyond[1], 12), ctx_swap(beside, 4)]
    parts = [slice(0, HEAD_DIM), slice(HEAD_DIM, 2 * HEAD_DIM)]
    key_grad, value_grad = [sum(array[:, p].astype(F32) for array in received).astype(BF16) for p in parts]
    return (query_grad, key_grad, value_grad)


def solution(mesh):
    return jax.shard_map(
        shards,
        mesh=mesh,
        in_specs=(
            P("ctx", "head"),
            P("ctx", "head"),
            P("ctx", "head"),
            P("ctx", "head"),
            P("head", None),
            P(),
            P(),
        ),
        out_specs=(P("ctx", "head"), P("ctx", "head"), P("ctx", "head")),
        check_vma=False,
    )
```
